128 devices in a mesh: ka: 16 (over z, y), wa: 8 (over x, core).
Axes of the slice: x: 4, y: 4, z: 4, core: 2. Of those that a mesh axis runs over, the one named last changes fastest.
Arguments:
- sigma_hist: bfloat16 [6, 2, 256, 153600], P(None, None, 'wa', 'ka'), may hold values from -6 to 6
- resid_hist: bfloat16 [6, 2, 256, 153600], P(None, None, 'wa', 'ka'), may hold values from -100 to 100
- sigma_new: bfloat16 [2, 256, 153600], P(None, 'wa', 'ka'), may hold values from -6 to 6
- resid_new: bfloat16 [2, 256, 153600], P(None, 'wa', 'ka'), may hold values from -100 to 100
- slot_order: int32 [6], replicated, may hold values from 0 to 5, each once
- freq_index: int32 [256], replicated, may hold values from -1024 to 1023, as said below
- freq_weight: float32 [256], replicated, may hold values from 0.02 to 0.2
Outputs:
- sigma_tau: float32 [256, 2, 153600], P(('ka', 'wa'))
- mixed_sigma: bfloat16 [2, 256, 153600], P(None, 'wa', 'ka')
- diis_coeffs: float32 [6], replicated
The draws below stay inside these ranges and needn't reach their ends.
Inputs may be any that keep to these rules, and one draw needn't show every extreme that they name: A permutation; slot_order[0] names the oldest slot. `freq_index`: distinct values; both -1024 and 1023 occur.
All inputs are finite; a program needn't handle non-finite values.
Results may differ from the reference program's by a relative error of at most 0.017.
Values may be sent and summed in bfloat16 or wider, within the bound.
A program may use at most 128 MiB of HBM per device.

```python
import math
import jax
import jax.numpy as jnp
from jax import lax

NORB = 200
NW = 256
NTAU = 256
NMAX = 1024
HIST = 6
KROWS = 768


def shared_parts(key, spread):
    gauss_key = jax.random.fold_in(key, 0)
    row_key = jax.random.fold_in(key, 2)
    col_key = jax.random.fold_in(key, 3)
    gaussian = jax.random.normal(gauss_key, (2, NW, KROWS, NORB), jnp.float32)
    common = jnp.clip(gaussian, -4.0, 4.0)
    row_scale = jnp.exp(jax.random.uniform(row_key, (KROWS,), jnp.float32, -spread, spread))
    col_scale = jnp.exp(jax.random.uniform(col_key, (2, NORB), jnp.float32, -spread, spread))
    return (common, row_scale, col_scale)


def shape_residual(common, private, row_scale, col_scale, slope_key, common_share):
    slot_count = private.shape[0]
    freq_key, row_key, first_sign, second_sign = jax.random.split(slope_key, 4)
    freq_slope = jax.random.uniform(freq_key, (slot_count,), jnp.float32, 0.55, 0.8)
    freq_slope = freq_slope * jnp.where(jax.random.uniform(first_sign, (slot_count,)) < 0.5, -1.0, 1.0)
    row_slope = jax.random.uniform(row_key, (slot_count,), jnp.float32, 0.55, 0.8)
    row_slope = row_slope * jnp.where(jax.random.uniform(second_sign, (slot_count,)) < 0.5, -1.0, 1.0)
    freq_pos = jnp.linspace(-1.0, 1.0, NW, dtype=jnp.float32)
    row_pos = jnp.linspace(-1.0, 1.0, KROWS, dtype=jnp.float32)
    growth = jnp.exp(freq_slope[:, None, None] * freq_pos[None, :, None] + row_slope[:, None, None] * row_pos[None, None, :])
    amplitude = 0.25 * growth[:, None, :, :, None] * row_scale[None, None, None, :, None] * col_scale[None, :, None, None, :]
    shaped = amplitude * (common_share ** 0.5 * common[None] + (1.0 - common_share) ** 0.5 * private)
    return shaped.reshape(slot_count, 2, NW, KROWS * NORB)


def draw_resid_hist(key, part):
    common, row_scale, col_scale = shared_parts(key, 1.15)
    key = jax.random.fold_in(key, 3)
    noise_key, slope_key = jax.random.split(key)
    private = jnp.clip(jax.random.normal(noise_key, (HIST, 2, NW, KROWS, NORB), jnp.float32), -4.0, 4.0)
    return shape_residual(common, private, row_scale, col_scale, slope_key, 0.5).astype(jnp.bfloat16)


def draw_resid_new(key, part):
    common, row_scale, col_scale = shared_parts(key, 1.15)
    key = jax.random.fold_in(key, 5)
    noise_key, slope_key = jax.random.split(key)
    private = jnp.clip(jax.random.normal(noise_key, (1, 2, NW, KROWS, NORB), jnp.float32), -4.0, 4.0)
    return shape_residual(common, private, row_scale, col_scale, slope_key, 0.5)[0].astype(jnp.bfloat16)


def draw_freq_index(key, part):
    key = jax.random.fold_in(key, 11)
    inner = jax.random.permutation(key, 2 * NMAX - 2)[:NW - 2].astype(jnp.int32) - (NMAX - 1)
    ends = jnp.array([-NMAX, NMAX - 1], jnp.int32)
    values = jnp.concatenate([ends, inner])
    placing = jax.random.permutation(jax.random.fold_in(key, 1), NW)
    return values[placing]


def steps_of(key, extent, cuts, low, top_value):
    def one(dim, shards_of):
        draws = jax.random.uniform(jax.random.fold_in(jax.random.fold_in(key, 6), dim), (shards_of,), jnp.float32, low / len(cuts), top_value / len(cuts))
        return jnp.repeat(jnp.exp(draws), extent[dim] // shards_of).reshape((-1,) + (1,) * (len(extent) - dim - 1))

    loudness = one(*cuts[0])
    for cut in cuts[1:]:
        loudness = loudness * one(*cut)
    return loudness


def normal_values(key, dims, width, reach, cuts=(), kind=jnp.bfloat16):
    drawn = jax.random.normal(key, dims, jnp.float32) * width
    if len(cuts) > 0:
        drawn = steps_of(key, dims, cuts, -0.22, 0.18) * drawn
    return jnp.clip(drawn, min=-reach, max=reach).astype(kind)


def setup_inputs(seed: int = 0) -> dict:
    keys = jax.random.split(jax.random.key(seed), 8)
    return {
        "sigma_hist": normal_values(keys[0], (HIST, 2, NW, KROWS * NORB), 1.0, 6.0, ((2, 8), (3, 16))),
        "resid_hist": draw_resid_hist(jax.random.fold_in(keys[7], 71), 0),
        "sigma_new": normal_values(keys[2], (2, NW, KROWS * NORB), 1.0, 6.0, ((1, 8), (2, 16))),
        "resid_new": draw_resid_new(jax.random.fold_in(keys[7], 71), 0),
        "slot_order": jax.random.permutation(keys[4], HIST).astype(jnp.int32),
        "freq_index": draw_freq_index(jax.random.fold_in(keys[7], 71), 0),
        "freq_weight": jnp.clip(jnp.exp(jax.random.uniform(keys[6], (NW,), jnp.float32, math.log(0.02), math.log(0.2))), 0.02, 0.2),
    }


def diis_weights(gram_matrix):
    factor = jnp.linalg.cholesky(gram_matrix)
    unit_vector = jnp.ones((gram_matrix.shape[0], 1), gram_matrix.dtype)
    halfway = lax.linalg.triangular_solve(factor, unit_vector, left_side=True, lower=True)
    solved = lax.linalg.triangular_solve(factor, halfway, left_side=True, lower=True, transpose_a=True)[:, 0]
    return solved / jnp.sum(solved)

def stacked_kernel(freq_index, freq_weight, tau_points, tau_count):
    odd_freq = 2 * freq_index + 1
    odd_tau = 2 * tau_points + 1
    phases = jnp.mod(odd_tau[:, None] * odd_freq[None, :], 4 * tau_count)
    angles = phases.astype(jnp.float32) * (math.pi / (2 * tau_count))
    kernel_re = (freq_weight[None, :] * jnp.cos(angles)).astype(jnp.bfloat16)
    kernel_im = (-freq_weight[None, :] * jnp.sin(angles)).astype(jnp.bfloat16)
    real_rows = jnp.concatenate([kernel_re, -kernel_im], axis=1)
    imag_rows = jnp.concatenate([kernel_im, kernel_re], axis=1)
    both = jnp.stack([real_rows, imag_rows], axis=1)
    return both.reshape(2 * tau_points.shape[0], 2 * freq_index.shape[0])

def apply_kernel(kernel, spectrum):
    flattened = spectrum.reshape(2 * spectrum.shape[1], spectrum.shape[2])
    result = jnp.dot(kernel.astype(jnp.float32), flattened.astype(jnp.float32), preferred_element_type=jnp.float32)
    return result.reshape(kernel.shape[0] // 2, 2, spectrum.shape[2])

def reference(sigma_hist, resid_hist, sigma_new, resid_new, slot_order, freq_index, freq_weight):
    chosen = jnp.arange(HIST, dtype=jnp.int32) == slot_order[0]
    freq_block = 8

    def gram_step(running, position):
        start_at = (position * freq_block).astype(jnp.int32)
        hist_part = lax.dynamic_slice_in_dim(resid_hist, start_at, freq_block, 2)
        new_part = lax.dynamic_slice_in_dim(resid_new, start_at, freq_block, 1)
        slot_block = jnp.where(chosen[:, None, None, None], new_part[None], hist_part)
        flattened = slot_block.reshape(HIST, -1)
        return (running + jnp.dot(flattened.astype(jnp.float32), flattened.T.astype(jnp.float32), preferred_element_type=jnp.float32), None)
    gram_matrix, _ = lax.scan(gram_step, jnp.zeros((HIST, HIST), jnp.float32), jnp.arange(NW // freq_block, dtype=jnp.int32))
    diis_coeffs = diis_weights(gram_matrix)
    summed = jnp.zeros(sigma_new.shape, jnp.float32)
    for member in range(HIST):
        sigma_slot = jnp.where(chosen[member], sigma_new, sigma_hist[member]).astype(jnp.float32)
        resid_slot = jnp.where(chosen[member], resid_new, resid_hist[member]).astype(jnp.float32)
        summed = summed + diis_coeffs[member] * (sigma_slot + resid_slot)
    mixed_sigma = summed.astype(jnp.bfloat16)
    kernel = stacked_kernel(freq_index, freq_weight, jnp.arange(NTAU, dtype=jnp.int32), NTAU)
    sigma_tau = apply_kernel(kernel, mixed_sigma)
    return (sigma_tau, mixed_sigma, diis_coeffs)
```

```python
import functools
import math

import jax
import jax.numpy as jnp
from jax import lax
from jax.experimental import pallas as pl
from jax.experimental.pallas import tpu as pltpu
from jax.sharding import PartitionSpec as P

MESH = pl.DeviceIdType.MESH
BF16, F32 = jnp.bfloat16, jnp.float32

HIST = 6
NTAU = 256
ROWS = 32
KA, WA = 16, 8
TILES = 75
UNIT = 512
WIDTH = TILES * 128
GRAM_PARTS = 5
EXTRA = 3
EXTRA_START = (64, 68, 71)
EXTRA_SLOTS = 6
GROUPS = 4
GROUP = KA // GROUPS


def sine(x):
    x2 = x * x
    p = -1.0 / 39916800.0
    for factor in (1.0 / 362880.0, -1.0 / 5040.0, 1.0 / 120.0, -1.0 / 6.0, 1.0):
        p = p * x2 + factor
    return x * p


def cosine_of_phase(phase):
    z = 256 - jnp.abs(phase - 512)
    return -sine(z.astype(F32) * (math.pi / 512))


def build_transform(freq_ref, weight_ref, table):
    odd_freq = 2 * freq_ref[...].reshape(1, NTAU) + 1
    weight = weight_ref[...].reshape(1, NTAU)

    def block(b, _):
        row = b * 64 + lax.broadcasted_iota(jnp.int32, (64, NTAU), 0)
        odd_tau = 2 * (row >> 1) + 1
        part = row & 1
        base = odd_freq * odd_tau + 256 * part
        for other in range(2):
            phase = (base - 256 * other) & 1023
            table[pl.ds(pl.multiple_of(b * 64, 64), 64), other * NTAU : (other + 1) * NTAU] = (
                weight * cosine_of_phase(phase)
            ).astype(BF16)
        return 0

    lax.fori_loop(0, 2 * NTAU // 64, block, 0)


def build_regroup(regroup):
    out = lax.broadcasted_iota(jnp.int32, (128, 128), 0)
    source = ((out >> 1) & 3) * 32 + (out >> 4) * 4 + ((out >> 3) & 1) * 2 + (out & 1)
    here = lax.broadcasted_iota(jnp.int32, (128, 128), 1)
    regroup[...] = jnp.where(source == here, 1.0, 0.0).astype(BF16)


def solve(gram, oldest):
    def entry(s, u):
        return jnp.broadcast_to(gram[s : s + 1, u : u + 1], (8, 128))

    full = {(s, u): entry(s, u) for s in range(HIST + 1) for u in range(s + 1)}
    mat = {}
    for s in range(HIST):
        for u in range(s + 1):
            value = jnp.where(oldest == s, full[HIST, u], full[s, u])
            if s == u:
                value = jnp.where(oldest == s, full[HIST, HIST], full[s, s])
            else:
                value = jnp.where(oldest == u, full[HIST, s], value)
            mat[s, u] = value
    low, inv = {}, {}
    for s in range(HIST):
        for u in range(s + 1):
            value = mat[s, u]
            for w in range(u):
                value = value - low[s, w] * low[u, w]
            if s == u:
                inv[s] = 1.0 / jnp.sqrt(value)
            else:
                low[s, u] = value * inv[u]
    half = {}
    for s in range(HIST):
        value = jnp.ones((8, 128), F32)
        for u in range(s):
            value = value - low[s, u] * half[u]
        half[s] = value * inv[s]
    full_solution = {}
    for s in reversed(range(HIST)):
        value = half[s]
        for u in range(s + 1, HIST):
            value = value - low[u, s] * full_solution[u]
        full_solution[s] = value * inv[s]
    total = full_solution[0]
    for s in range(1, HIST):
        total = total + full_solution[s]
    return [full_solution[s] / total for s in range(HIST)]


def main_kernel(
    slot_ref, freq_ref, weight_ref, sig_hist, res_hist, sig_new, res_new,
    own, own_extra, mixed_out, coef_out,
    sig_v, res_v, sign_v, resn_v, weights, gx, gy, table, regroup,
    mixed, spectra, turned, spread, spread_extra,
    in_sem, gs_sem, gr_sem, s1, r1, s2, r2, s3, r3, out_sem, local_sem,
):
    k, i = lax.axis_index("ka"), lax.axis_index("wa")
    x, core = i // 2, i % 2
    z, y = k // 4, k % 4

    part = WIDTH // GRAM_PARTS
    reads = []
    for n in range(GRAM_PARTS):
        cols = pl.ds(n * part, part)
        reads.append(
            (
                pltpu.make_async_copy(res_hist.at[:, :, :, cols], res_v.at[:, :, :, cols], in_sem.at[0, n]),
                pltpu.make_async_copy(res_new.at[:, :, cols], resn_v.at[:, :, cols], in_sem.at[1, n]),
            )
        )
    sigma_reads = []
    for n, (start, size) in enumerate(((8192, 1408), (0, 4096), (4096, 4096))):
        cols = pl.ds(start, size)
        sigma_reads.append(
            (
                pltpu.make_async_copy(sig_hist.at[:, :, :, cols], sig_v.at[:, :, :, cols], in_sem.at[2, n]),
                pltpu.make_async_copy(sig_new.at[:, :, cols], sign_v.at[:, :, cols], in_sem.at[3, n]),
            )
        )
    for pair in reads + sigma_reads:
        for read in pair:
            read.start()

    barrier = pltpu.get_barrier_semaphore()

    def greet_wa(d, _):
        pl.semaphore_signal(barrier, inc=1, device_id=(k, (i + d) % WA), device_id_type=MESH)
        return 0

    def greet_ka(d, _):
        pl.semaphore_signal(barrier, inc=1, device_id=((k + d) % KA, i), device_id_type=MESH)
        return 0

    lax.fori_loop(1, WA, greet_wa, 0)
    lax.fori_loop(1, KA, greet_ka, 0)

    acc = jnp.zeros((7 * ROWS, 7 * ROWS), F32)
    for n in range(GRAM_PARTS):
        for read in reads[n]:
            read.wait()
        for ri in range(2):
            block = jnp.concatenate(
                [
                    res_v[:, ri, :, n * part : (n + 1) * part].reshape(HIST * ROWS, part),
                    resn_v[ri, :, n * part : (n + 1) * part],
                ],
                axis=0,
            )
            acc = acc + lax.dot_general(block, block, (((1,), (1,)), ((), ())), preferred_element_type=F32)
    rows = lax.broadcasted_iota(jnp.int32, acc.shape, 0)
    lanes = lax.broadcasted_iota(jnp.int32, acc.shape, 1)
    kept = jnp.where((rows & (ROWS - 1)) == (lanes & (ROWS - 1)), acc, 0.0)
    by_lane = jnp.sum(kept.reshape(7, ROWS, 7 * ROWS), axis=1)
    fold = jnp.where(
        lax.broadcasted_iota(jnp.int32, (7 * ROWS, 128), 0) // ROWS
        == lax.broadcasted_iota(jnp.int32, (7 * ROWS, 128), 1),
        1.0,
        0.0,
    )
    share = jnp.dot(by_lane, fold, preferred_element_type=F32, precision=lax.Precision.HIGHEST)
    gx[i] = jnp.concatenate([share, jnp.zeros((1, 128), F32)], axis=0)

    pl.semaphore_wait(barrier, WA - 1 + KA - 1)

    def share_wa(d):
        return pltpu.make_async_remote_copy(
            src_ref=gx.at[i], dst_ref=gx.at[i], send_sem=gs_sem.at[0, d], recv_sem=gr_sem.at[0, d],
            device_id=(k, (i + d) % WA), device_id_type=MESH)

    def share_ka(d):
        return pltpu.make_async_remote_copy(
            src_ref=gy.at[k], dst_ref=gy.at[k], send_sem=gs_sem.at[1, d], recv_sem=gr_sem.at[1, d],
            device_id=((k + d) % KA, i), device_id_type=MESH)

    def each(low, high, do):
        def step(d, _):
            do(d)
            return 0

        lax.fori_loop(low, high, step, 0)

    each(1, WA, lambda d: share_wa(d).start())
    build_transform(freq_ref, weight_ref, table)
    build_regroup(regroup)
    each(1, WA, lambda d: share_wa(d).wait())
    total = gx[0]
    for n in range(1, WA):
        total = total + gx[n]
    gy[k] = total
    each(1, KA, lambda d: share_ka(d).start())
    each(1, KA, lambda d: share_ka(d).wait())
    gram = gy[0]
    for n in range(1, KA):
        gram = gram + gy[n]

    oldest = slot_ref[0]
    coeffs = solve(gram, oldest)
    lane = lax.broadcasted_iota(jnp.int32, (8, 128), 1)
    packed = jnp.zeros((8, 128), F32)
    newest = jnp.zeros((8, 128), F32)
    for s in range(HIST):
        packed = jnp.where(lane == s, coeffs[s], packed)
        newest = jnp.where(oldest == s, coeffs[s], newest)
        weights[s] = jnp.where(oldest == s, 0.0, coeffs[s])
    weights[HIST] = newest
    coef_out[...] = packed

    def mix(unit, start):
        def rows_of(h, _):
            ri, low = h // 2, pl.multiple_of((h % 2) * 16, 16)
            for tile in range(4):
                cols = pl.ds(pl.multiple_of(start + tile * 128, 128), 128)
                at = (ri, pl.ds(low, 16), cols)
                w = weights[HIST]
                both = jnp.concatenate([w, w], axis=0)
                total = both * (sign_v[at].astype(F32) + resn_v[at].astype(F32))
                for s in range(HIST):
                    w = weights[s]
                    both = jnp.concatenate([w, w], axis=0)
                    total = total + both * (sig_v[(s, *at)].astype(F32) + res_v[(s, *at)].astype(F32))
                mixed[unit, ri, pl.ds(low, 16), tile * 128 : (tile + 1) * 128] = total.astype(BF16)
            return 0

        lax.fori_loop(0, 4, rows_of, 0)

    def unit_copy(c, d):
        j = (i + d) % WA
        return pltpu.make_async_remote_copy(
            src_ref=mixed.at[c * WA + j], dst_ref=spectra.at[c, :, i],
            send_sem=s1.at[c, d], recv_sem=r1.at[c, d], device_id=(k, j), device_id_type=MESH)

    def unit_keep(c):
        return pltpu.make_async_copy(mixed.at[c * WA + i], spectra.at[c, :, i], local_sem.at[0, c])

    def owner_of(m):
        return 2 * ((m + y) % 4) + z % 2

    def extra_copy(m):
        return pltpu.make_async_remote_copy(
            src_ref=mixed.at[2 * WA + m], dst_ref=spectra.at[2, :, i],
            send_sem=s1.at[2, m], recv_sem=r1.at[2, i], device_id=(k, owner_of(m)), device_id_type=MESH)

    def extra_keep(m):
        return pltpu.make_async_copy(mixed.at[2 * WA + m], spectra.at[2, :, i], local_sem.at[0, 2])

    def extra_arrival(n):
        return pltpu.make_async_remote_copy(
            src_ref=mixed.at[2 * WA], dst_ref=spectra.at[2, :, n],
            send_sem=s1.at[2, 0], recv_sem=r1.at[2, n], device_id=(k, n), device_id_type=MESH)

    writes = []
    for n, (unit, skip) in enumerate([(u, 0) for u in range(18)] + [(18, 128)]):
        start = unit * UNIT if unit < 16 else EXTRA_START[unit - 16] * 128
        writes.append(
            pltpu.make_async_copy(
                mixed.at[unit, :, :, skip:UNIT],
                mixed_out.at[:, :, start + skip : start + UNIT],
                out_sem.at[n],
            )
        )

    for read in sigma_reads[0]:
        read.wait()
    for m in range(EXTRA):
        mix(2 * WA + m, EXTRA_START[m] * 128)

        @pl.when(owner_of(m) == i)
        def _(m=m):
            extra_keep(m).start()

        @pl.when(owner_of(m) != i)
        def _(m=m):
            extra_copy(m).start()

    for c in range(2):
        for read in sigma_reads[1 + c]:
            read.wait()

        def send_unit(d, c=c):
            unit = c * WA + (i + d) % WA
            mix(unit, unit * UNIT)

            @pl.when(d == 0)
            def _():
                unit_keep(c).start()

            @pl.when(d != 0)
            def _():
                unit_copy(c, d).start()

        each(0, WA, send_unit)
    for write in writes:
        write.start()

    def transform(c):
        values = jnp.dot(table[...], spectra[c].reshape(2 * NTAU, UNIT), preferred_element_type=F32).astype(BF16)
        for b in range(4):
            stacked = jnp.concatenate(
                [
                    jnp.concatenate(
                        [values[(4 * b + n) * 32 : (4 * b + n + 1) * 32, a * 128 : (a + 1) * 128] for a in range(4)],
                        axis=0,
                    )
                    for n in range(4)
                ],
                axis=1,
            )
            grouped = jnp.dot(regroup[...], stacked, preferred_element_type=F32).astype(BF16)
            for n in range(4):
                turned[c, 4 * b + n] = grouped[:, n * 128 : (n + 1) * 128].reshape(WA, 16, 128)

    def times_copy(c, d):
        peer = (k + d) % KA
        return pltpu.make_async_remote_copy(
            src_ref=turned.at[c, peer], dst_ref=spread.at[c, d],
            send_sem=s2.at[c, d], recv_sem=r2.at[c, d], device_id=(peer, i), device_id_type=MESH)

    def times_keep(c):
        return pltpu.make_async_copy(turned.at[c, k], spread.at[c, 0], local_sem.at[1, c])

    extra_m = (x - y + 4) % 4
    is_owner = jnp.logical_and(z % 2 == core, extra_m < EXTRA)
    my_slot = (z // 2) * EXTRA + extra_m

    def slot_source(s):
        return 4 * (2 * (s // EXTRA) + core) + (x - s % EXTRA + 4) % 4

    def extra_times_copy(d):
        peer = (k + d) % KA
        return pltpu.make_async_remote_copy(
            src_ref=turned.at[2, peer], dst_ref=spread_extra.at[my_slot],
            send_sem=s2.at[2, d], recv_sem=r2.at[2, my_slot], device_id=(peer, i), device_id_type=MESH)

    def extra_times_keep():
        return pltpu.make_async_copy(turned.at[2, k], spread_extra.at[my_slot], local_sem.at[1, 2])

    def extra_times_arrival(s):
        return pltpu.make_async_remote_copy(
            src_ref=turned.at[2, 0], dst_ref=spread_extra.at[s],
            send_sem=s2.at[2, 0], recv_sem=r2.at[2, s], device_id=(slot_source(s), i), device_id_type=MESH)

    def owner_copy(c, g, e):
        j = (i + e) % WA
        ds = pl.ds(g * GROUP, GROUP)
        return pltpu.make_async_remote_copy(
            src_ref=spread.at[c, ds, j], dst_ref=own.at[c, i, ds],
            send_sem=s3.at[c, g, e], recv_sem=r3.at[c, g, e], device_id=(k, j), device_id_type=MESH)

    def owner_keep(c, g):
        ds = pl.ds(g * GROUP, GROUP)
        return pltpu.make_async_copy(spread.at[c, ds, i], own.at[c, i, ds], s3.at[c, g, 0])

    def extra_owner_copy(e):
        j = (i + e) % WA
        return pltpu.make_async_remote_copy(
            src_ref=spread_extra.at[:, j], dst_ref=own_extra.at[i],
            send_sem=s3.at[2, 0, e], recv_sem=r3.at[2, 0, e], device_id=(k, j), device_id_type=MESH)

    def extra_owner_keep():
        return pltpu.make_async_copy(spread_extra.at[:, i], own_extra.at[i], s3.at[2, 0, 0])

    @pl.when(is_owner)
    def _():
        extra_keep(0).wait()
        for d in range(1, WA):
            extra_arrival((i + d) % WA).wait_recv()
        transform(2)
        extra_times_keep().start()
        each(1, KA, lambda d: extra_times_copy(d).start())

    def first_stage(c):
        unit_keep(c).wait()
        each(1, WA, lambda d: unit_copy(c, d).wait_recv())
        transform(c)
        times_keep(c).start()
        each(1, KA, lambda d: times_copy(c, d).start())

    def last_stage(c):
        times_keep(c).wait()

        def group(g):
            def arrived(d):
                @pl.when(d != 0)
                def _():
                    times_copy(c, d).wait_recv()

            each(g * GROUP, (g + 1) * GROUP, arrived)
            each(1, WA, lambda e: owner_copy(c, g, e).start())
            owner_keep(c, g).start()

        each(0, GROUPS, group)

    first_stage(0)

    @pl.when(is_owner)
    def _():
        extra_times_keep().wait()

    def extra_arrived(s):
        @pl.when(slot_source(s) != k)
        def _():
            extra_times_arrival(s).wait_recv()

    each(0, EXTRA_SLOTS, extra_arrived)
    each(1, WA, lambda e: extra_owner_copy(e).start())
    extra_owner_keep().start()

    first_stage(1)
    last_stage(0)
    last_stage(1)

    for m in range(EXTRA):

        @pl.when(owner_of(m) != i)
        def _(m=m):
            extra_copy(m).wait_send()

    for c in range(2):
        each(1, WA, lambda d, c=c: unit_copy(c, d).wait_send())
        each(1, KA, lambda d, c=c: times_copy(c, d).wait_send())

    @pl.when(is_owner)
    def _():
        each(1, KA, lambda d: extra_times_copy(d).wait_send())

    for write in writes:
        write.wait()
    extra_owner_keep().wait()
    each(1, WA, lambda e: extra_owner_copy(e).wait())
    for c in range(2):

        def finish(g, c=c):
            owner_keep(c, g).wait()
            each(1, WA, lambda e: owner_copy(c, g, e).wait())

        each(0, GROUPS, finish)


def last_kernel(own, own_extra, mixed_in, coef_in, out, mixed_out, coef_out, times, out_sem):
    k, i = lax.axis_index("ka"), lax.axis_index("wa")
    passed = pltpu.make_async_copy(mixed_in, mixed_out, out_sem.at[2])
    passed.start()
    coef_out[...] = coef_in[0, :HIST]

    def place(value, tile):
        value = value.astype(F32)
        at = pl.ds(2 * tile, 8)
        times[0, at] = value[:8]
        times[1, at] = value[8:]

    def from_row(d, _):
        row = (k - d + KA) % KA
        for c in range(2):
            for n in range(WA):
                place(own[c, n, d], row * TILES + (c * WA + n) * 4)
        return 0

    lax.fori_loop(0, KA, from_row, 0)

    for n in range(WA):
        x, core = n // 2, n % 2
        for s in range(EXTRA_SLOTS):
            m = s % EXTRA
            row = 4 * (2 * (s // EXTRA) + core) + (x - m) % 4
            place(own_extra[n, s], row * TILES + EXTRA_START[m])
    writes = [pltpu.make_async_copy(times.at[t], out.at[t], out_sem.at[t]) for t in range(2)]
    for write in writes:
        write.start()
    for write in writes:
        write.wait()
    passed.wait()


def shards(sigma_hist, resid_hist, sigma_new, resid_new, slot_order, freq_index, freq_weight):
    vmem = pl.BlockSpec(memory_space=pltpu.VMEM)
    hbm = pl.BlockSpec(memory_space=pl.ANY)
    smem = pl.BlockSpec(memory_space=pltpu.SMEM)
    dma = pltpu.SemaphoreType.DMA
    own, own_extra, mixed, coeffs = pl.pallas_call(
        main_kernel,
        out_shape=(
            jax.ShapeDtypeStruct((2, WA, KA, 16, 128), BF16),
            jax.ShapeDtypeStruct((WA, EXTRA_SLOTS, 16, 128), BF16),
            jax.ShapeDtypeStruct(sigma_new.shape, BF16),
            jax.ShapeDtypeStruct((8, 128), F32),
        ),
        in_specs=[smem, vmem, vmem, hbm, hbm, hbm, hbm],
        out_specs=(hbm, hbm, hbm, vmem),
        scratch_shapes=[
            pltpu.VMEM(sigma_hist.shape, BF16),
            pltpu.VMEM(resid_hist.shape, BF16),
            pltpu.VMEM(sigma_new.shape, BF16),
            pltpu.VMEM(resid_new.shape, BF16),
            pltpu.VMEM((HIST + 1, 8, 128), F32),
            pltpu.VMEM((WA, 8, 128), F32),
            pltpu.VMEM((KA, 8, 128), F32),
            pltpu.VMEM((2 * NTAU, 2 * NTAU), BF16),
            pltpu.VMEM((128, 128), BF16),
            pltpu.VMEM((2 * WA + EXTRA, 2, ROWS, UNIT), BF16),
            pltpu.VMEM((3, 2, WA, ROWS, UNIT), BF16),
            pltpu.VMEM((3, KA, WA, 16, 128), BF16),
            pltpu.VMEM((2, KA, WA, 16, 128), BF16),
            pltpu.VMEM((EXTRA_SLOTS, WA, 16, 128), BF16),
            dma((4, GRAM_PARTS)),
            dma((2, KA)),
            dma((2, KA)),
            dma((3, WA)),
            dma((3, WA)),
            dma((3, KA)),
            dma((3, KA)),
            dma((3, GROUPS, WA)),
            dma((3, GROUPS, WA)),
            dma((2 * WA + EXTRA,)),
            dma((2, 3)),
        ],
        compiler_params=pltpu.CompilerParams(
            collective_id=0, has_side_effects=True, vmem_limit_bytes=48 * 2**20
        ),
        name="mix_and_transform",
    )(slot_order, freq_index, freq_weight, sigma_hist, resid_hist, sigma_new, resid_new)
    out, mixed_sigma, diis_coeffs = pl.pallas_call(
        last_kernel,
        out_shape=(
            jax.ShapeDtypeStruct((2, KA * TILES * 2, 128), F32),
            jax.ShapeDtypeStruct(sigma_new.shape, BF16),
            jax.ShapeDtypeStruct((HIST,), F32),
        ),
        in_specs=[vmem, vmem, hbm, vmem],
        out_specs=(hbm, hbm, vmem),
        scratch_shapes=[pltpu.VMEM((2, KA * TILES * 2, 128), F32), dma((3,))],
        compiler_params=pltpu.CompilerParams(vmem_limit_bytes=16 * 2**20),
        name="unpack",
    )(own, own_extra, mixed, coeffs)
    sigma_tau = out.reshape(2, KA * TILES, 2, 128).transpose(0, 2, 1, 3).reshape(2, 2, KA * WIDTH)
    return (sigma_tau, mixed_sigma, diis_coeffs)


def solution(mesh):
    return jax.shard_map(
        shards,
        mesh=mesh,
        in_specs=(
            P(None, None, "wa", "ka"),
            P(None, None, "wa", "ka"),
            P(None, "wa", "ka"),
            P(None, "wa", "ka"),
            P(),
            P(),
            P(),
        ),
        out_specs=(P(("ka", "wa"), None, None), P(None, "wa", "ka"), P()),
        check_vma=False,
    )
```

```python
import functools
import math

import jax
import jax.numpy as jnp
from jax import lax
from jax.experimental import pallas as pl
from jax.experimental.pallas import tpu as pltpu
from jax.sharding import PartitionSpec as P

MESH = pl.DeviceIdType.MESH
BF16, F32 = jnp.bfloat16, jnp.float32

HIST = 6
NTAU = 256
ROWS = 32
KA, WA = 16, 8
TILES = 75
UNIT = 512
WIDTH = TILES * 128
GRAM_PARTS = ((0, 50), (50, 25))
GRAM_STEP = 25
EXTRA = 3
EXTRA_START = (64, 68, 71)
EXTRA_SLOTS = 6
GROUPS = 4
GROUP = KA // GROUPS
OFFSETS = ((2, 2), (2, 1), (2, 3), (2, 0), (1, 2), (3, 2), (1, 1), (3, 3), (1, 3), (3, 1), (1, 0), (3, 0), (0, 2), (0, 1), (0, 3))
GROUP_ORDER = (2, 1, 3, 0)


def sine(x):
    x2 = x * x
    p = -1.0 / 39916800.0
    for factor in (1.0 / 362880.0, -1.0 / 5040.0, 1.0 / 120.0, -1.0 / 6.0, 1.0):
        p = p * x2 + factor
    return x * p


def cosine_of_phase(phase):
    z = 256 - jnp.abs(phase - 512)
    return -sine(z.astype(F32) * (math.pi / 512))


def build_transform(small, table):
    odd_freq = 2 * jnp.concatenate([small[0:1], small[1:2]], axis=1).astype(jnp.int32) + 1
    weight = jnp.concatenate([small[2:3], small[3:4]], axis=1)

    def block(b, _):
        row = b * 64 + lax.broadcasted_iota(jnp.int32, (64, NTAU), 0)
        odd_tau = 2 * (row >> 1) + 1
        part = row & 1
        base = odd_freq * odd_tau + 256 * part
        for other in range(2):
            phase = (base - 256 * other) & 1023
            table[pl.ds(pl.multiple_of(b * 64, 64), 64), other * NTAU : (other + 1) * NTAU] = (
                weight * cosine_of_phase(phase)
            ).astype(BF16)
        return 0

    lax.fori_loop(0, 2 * NTAU // 64, block, 0)


def build_regroup(regroup):
    out = lax.broadcasted_iota(jnp.int32, (128, 128), 0)
    source = ((out >> 1) & 3) * 32 + (out >> 4) * 4 + ((out >> 3) & 1) * 2 + (out & 1)
    here = lax.broadcasted_iota(jnp.int32, (128, 128), 1)
    regroup[...] = jnp.where(source == here, 1.0, 0.0).astype(BF16)


def solve(gram, oldest):
    def entry(s, u):
        return jnp.broadcast_to(gram[s : s + 1, u : u + 1], (8, 128))

    full = {(s, u): entry(s, u) for s in range(HIST + 1) for u in range(s + 1)}
    mat = {}
    for s in range(HIST):
        for u in range(s + 1):
            value = jnp.where(oldest == s, full[HIST, u], full[s, u])
            if s == u:
                value = jnp.where(oldest == s, full[HIST, HIST], full[s, s])
            else:
                value = jnp.where(oldest == u, full[HIST, s], value)
            mat[s, u] = value
    low, inv = {}, {}
    for s in range(HIST):
        for u in range(s + 1):
            value = mat[s, u]
            for w in range(u):
                value = value - low[s, w] * low[u, w]
            if s == u:
                inv[s] = 1.0 / jnp.sqrt(value)
            else:
                low[s, u] = value * inv[u]
    half = {}
    for s in range(HIST):
        value = jnp.ones((8, 128), F32)
        for u in range(s):
            value = value - low[s, u] * half[u]
        half[s] = value * inv[s]
    full_solution = {}
    for s in reversed(range(HIST)):
        value = half[s]
        for u in range(s + 1, HIST):
            value = value - low[u, s] * full_solution[u]
        full_solution[s] = value * inv[s]
    total = full_solution[0]
    for s in range(1, HIST):
        total = total + full_solution[s]
    return [full_solution[s] / total for s in range(HIST)]


def main_kernel(
    small, sig_hist, res_hist, sig_new, res_new,
    own, own_extra, mixed_out, coef_out,
    sig_v, res_v, sign_v, resn_v, acc, weights, gx, gy, table, regroup,
    mixed, spectra, turned, spread, spread_extra,
    in_sem, share_sem, s1, r1, se, s2, r2, r2e, s3, r3, out_sem, local_sem,
):
    k, i = lax.axis_index("ka"), lax.axis_index("wa")
    x, core = i // 2, i % 2
    z, y = k // 4, k % 4

    def each(low, high, do):
        def step(d, _):
            do(d)
            return 0

        lax.fori_loop(low, high, step, 0)

    def arrived(ref, sem):
        pltpu.make_async_copy(ref, ref, sem).wait()

    reads = []
    for n, (start, size) in enumerate(GRAM_PARTS):
        cols = pl.ds(start * 128, size * 128)
        reads.append(
            (
                pltpu.make_async_copy(res_hist.at[:, :, :, cols], res_v.at[:, :, :, cols], in_sem.at[0, n]),
                pltpu.make_async_copy(res_new.at[:, :, cols], resn_v.at[:, :, cols], in_sem.at[1, n]),
            )
        )
    sigma_reads = []
    for n, (start, size) in enumerate(((8192, 1408), (0, 4096), (4096, 4096))):
        cols = pl.ds(start, size)
        sigma_reads.append(
            (
                pltpu.make_async_copy(sig_hist.at[:, :, :, cols], sig_v.at[:, :, :, cols], in_sem.at[2, n]),
                pltpu.make_async_copy(sig_new.at[:, :, cols], sign_v.at[:, :, cols], in_sem.at[3, n]),
            )
        )
    for group in reads:
        for read in group:
            read.start()

    barrier = pltpu.get_barrier_semaphore()

    def greet_wa(d, _):
        pl.semaphore_signal(barrier, inc=1, device_id=(k, (i + d) % WA), device_id_type=MESH)
        return 0

    def greet_ka(d, _):
        pl.semaphore_signal(barrier, inc=1, device_id=((k + d) % KA, i), device_id_type=MESH)
        return 0

    lax.fori_loop(1, WA, greet_wa, 0)
    lax.fori_loop(1, KA, greet_ka, 0)

    acc[...] = jnp.zeros_like(acc)
    for n, (start, size) in enumerate(GRAM_PARTS):
        for read in reads[n]:
            read.wait()

        def add_products(b, start=start):
            cols = pl.ds(pl.multiple_of((start + b * GRAM_STEP) * 128, 128), GRAM_STEP * 128)
            total = None
            for ri in range(2):
                block = jnp.concatenate(
                    [res_v[:, ri, :, cols].reshape(HIST * ROWS, GRAM_STEP * 128), resn_v[ri, :, cols]], axis=0
                )
                product = lax.dot_general(block, block, (((1,), (1,)), ((), ())), preferred_element_type=F32)
                total = product if total is None else total + product
            acc[...] += total

        each(0, size // GRAM_STEP, add_products)
    for pair in sigma_reads:
        for read in pair:
            read.start()
    rows = lax.broadcasted_iota(jnp.int32, acc.shape, 0)
    lanes = lax.broadcasted_iota(jnp.int32, acc.shape, 1)
    kept = jnp.where((rows & (ROWS - 1)) == (lanes & (ROWS - 1)), acc[...], 0.0)
    by_lane = jnp.sum(kept.reshape(7, ROWS, 7 * ROWS), axis=1)
    fold = jnp.where(
        lax.broadcasted_iota(jnp.int32, (7 * ROWS, 128), 0) // ROWS
        == lax.broadcasted_iota(jnp.int32, (7 * ROWS, 128), 1),
        1.0,
        0.0,
    )
    share = jnp.dot(by_lane, fold, preferred_element_type=F32, precision=lax.Precision.HIGHEST)
    gx[i] = jnp.concatenate([share, jnp.zeros((1, 128), F32)], axis=0)

    pl.semaphore_wait(barrier, WA - 1 + KA - 1)

    def share_wa(d):
        return pltpu.make_async_remote_copy(
            src_ref=gx.at[i], dst_ref=gx.at[i], send_sem=share_sem.at[0], recv_sem=share_sem.at[1],
            device_id=(k, (i + d) % WA), device_id_type=MESH)

    def share_ka(d):
        return pltpu.make_async_remote_copy(
            src_ref=gy.at[k], dst_ref=gy.at[k], send_sem=share_sem.at[2], recv_sem=share_sem.at[3],
            device_id=((k + d) % KA, i), device_id_type=MESH)

    each(1, WA, lambda d: share_wa(d).start())
    build_transform(small, table)
    build_regroup(regroup)
    for n in range(2):
        arrived(gx.at[: WA - 1], share_sem.at[n])
    total = gx[0]
    for n in range(1, WA):
        total = total + gx[n]
    gy[k] = total
    each(1, KA, lambda d: share_ka(d).start())
    for n in range(2, 4):
        arrived(gy.at[: KA - 1], share_sem.at[n])
    gram = gy[0]
    for n in range(1, KA):
        gram = gram + gy[n]

    oldest = jnp.broadcast_to(small[4:5, 0:1], (8, 128))
    coeffs = solve(gram, oldest)
    lane = lax.broadcasted_iota(jnp.int32, (8, 128), 1)
    packed = jnp.zeros((8, 128), F32)
    newest = jnp.zeros((8, 128), F32)
    for s in range(HIST):
        packed = jnp.where(lane == s, coeffs[s], packed)
        newest = jnp.where(oldest == s, coeffs[s], newest)
        weights[s] = jnp.where(oldest == s, 0.0, coeffs[s])
    weights[HIST] = newest
    coef_out[...] = packed

    def mix(unit, start):
        def rows_of(h, _):
            ri, low = h // 2, pl.multiple_of((h % 2) * 16, 16)
            for tile in range(4):
                cols = pl.ds(pl.multiple_of(start + tile * 128, 128), 128)
                at = (ri, pl.ds(low, 16), cols)
                w = weights[HIST]
                both = jnp.concatenate([w, w], axis=0)
                total = both * (sign_v[at].astype(F32) + resn_v[at].astype(F32))
                for s in range(HIST):
                    w = weights[s]
                    both = jnp.concatenate([w, w], axis=0)
                    total = total + both * (sig_v[(s, *at)].astype(F32) + res_v[(s, *at)].astype(F32))
                mixed[unit, ri, pl.ds(low, 16), tile * 128 : (tile + 1) * 128] = total.astype(BF16)
            return 0

        lax.fori_loop(0, 4, rows_of, 0)

    def unit_copy(c, d):
        j = (i + d) % WA
        return pltpu.make_async_remote_copy(
            src_ref=mixed.at[c * WA + j], dst_ref=spectra.at[c, :, i],
            send_sem=s1.at[c], recv_sem=r1.at[c], device_id=(k, j), device_id_type=MESH)

    def unit_keep(c):
        return pltpu.make_async_copy(mixed.at[c * WA + i], spectra.at[c, :, i], local_sem.at[0, c])

    def owner_of(m):
        return 2 * ((m + y) % 4) + z % 2

    def extra_copy(m):
        return pltpu.make_async_remote_copy(
            src_ref=mixed.at[2 * WA + m], dst_ref=spectra.at[2, :, i],
            send_sem=se.at[m], recv_sem=r1.at[2], device_id=(k, owner_of(m)), device_id_type=MESH)

    def extra_keep(m):
        return pltpu.make_async_copy(mixed.at[2 * WA + m], spectra.at[2, :, i], local_sem.at[0, 2])

    writes = []
    for unit, skip in [(u, 0) for u in range(18)] + [(18, 128)]:
        start = unit * UNIT if unit < 16 else EXTRA_START[unit - 16] * 128
        writes.append(
            pltpu.make_async_copy(
                mixed.at[unit, :, :, skip:UNIT],
                mixed_out.at[:, :, start + skip : start + UNIT],
                out_sem,
            )
        )

    for read in sigma_reads[0]:
        read.wait()
    for m in range(EXTRA):
        mix(2 * WA + m, EXTRA_START[m] * 128)

        @pl.when(owner_of(m) == i)
        def _(m=m):
            extra_keep(m).start()

        @pl.when(owner_of(m) != i)
        def _(m=m):
            extra_copy(m).start()

    for c in range(2):
        for read in sigma_reads[1 + c]:
            read.wait()

        def send_unit(d, c=c):
            unit = c * WA + (i + d) % WA
            mix(unit, unit * UNIT)

            @pl.when(d == 0)
            def _():
                unit_keep(c).start()

            @pl.when(d != 0)
            def _():
                unit_copy(c, d).start()

        each(0, WA, send_unit)
    for write in writes:
        write.start()

    def transform(c):
        def block(b):
            values = jnp.dot(
                table[pl.ds(pl.multiple_of(b * 128, 128), 128)],
                spectra[c].reshape(2 * NTAU, UNIT),
                preferred_element_type=F32,
            ).astype(BF16)
            stacked = jnp.concatenate(
                [
                    jnp.concatenate(
                        [values[n * 32 : (n + 1) * 32, a * 128 : (a + 1) * 128] for a in range(4)], axis=0
                    )
                    for n in range(4)
                ],
                axis=1,
            )
            grouped = jnp.dot(regroup[...], stacked, preferred_element_type=F32).astype(BF16)
            for n in range(4):
                turned[c, 4 * b + n] = grouped[:, n * 128 : (n + 1) * 128].reshape(WA, 16, 128)

        each(0, 4, block)

    def peer_at(d):
        return (z + d // 4) % 4 * 4 + (y + d % 4) % 4

    def times_copy(c, d):
        peer = peer_at(d)
        return pltpu.make_async_remote_copy(
            src_ref=turned.at[c, peer], dst_ref=spread.at[c, d],
            send_sem=s2.at[c], recv_sem=r2.at[c, d // GROUP], device_id=(peer, i), device_id_type=MESH)

    def times_keep(c):
        return pltpu.make_async_copy(turned.at[c, k], spread.at[c, 0], local_sem.at[1, c])

    extra_m = (x - y + 4) % 4
    is_owner = jnp.logical_and(z % 2 == core, extra_m < EXTRA)
    my_slot = (z // 2) * EXTRA + extra_m

    def slot_source(s):
        return 4 * (2 * (s // EXTRA) + core) + (x - s % EXTRA + 4) % 4

    def extra_times_copy(d):
        peer = peer_at(d)
        return pltpu.make_async_remote_copy(
            src_ref=turned.at[2, peer], dst_ref=spread_extra.at[my_slot],
            send_sem=s2.at[2], recv_sem=r2e.at[my_slot], device_id=(peer, i), device_id_type=MESH)

    def extra_times_keep():
        return pltpu.make_async_copy(turned.at[2, k], spread_extra.at[my_slot], local_sem.at[1, 2])

    def extra_times_arrival(s):
        return pltpu.make_async_remote_copy(
            src_ref=turned.at[2, 0], dst_ref=spread_extra.at[s],
            send_sem=s2.at[2], recv_sem=r2e.at[s], device_id=(slot_source(s), i), device_id_type=MESH)

    def owner_copy(c, g, e):
        j = (i + e) % WA
        ds = pl.ds(g * GROUP, GROUP)
        return pltpu.make_async_remote_copy(
            src_ref=spread.at[c, ds, j], dst_ref=own.at[c, i, ds],
            send_sem=s3.at[c], recv_sem=r3.at[c], device_id=(k, j), device_id_type=MESH)

    def owner_keep(c, g):
        ds = pl.ds(g * GROUP, GROUP)
        return pltpu.make_async_copy(spread.at[c, ds, i], own.at[c, i, ds], local_sem.at[2, c])

    def extra_owner_copy(e):
        j = (i + e) % WA
        return pltpu.make_async_remote_copy(
            src_ref=spread_extra.at[:, j], dst_ref=own_extra.at[i],
            send_sem=s3.at[2], recv_sem=r3.at[2], device_id=(k, j), device_id_type=MESH)

    def extra_owner_keep():
        return pltpu.make_async_copy(spread_extra.at[:, i], own_extra.at[i], local_sem.at[2, 2])

    @pl.when(is_owner)
    def _():
        extra_keep(0).wait()
        arrived(spectra.at[2, :, : WA - 1], r1.at[2])
        transform(2)
        extra_times_keep().start()
        for dz, dy in OFFSETS:
            extra_times_copy(dz * 4 + dy).start()

    def first_stage(c):
        unit_keep(c).wait()
        arrived(spectra.at[c, :, : WA - 1], r1.at[c])
        transform(c)
        times_keep(c).start()
        for dz, dy in OFFSETS:
            times_copy(c, dz * 4 + dy).start()

    def last_stage(c):
        for g in GROUP_ORDER:
            if g == 0:
                times_keep(c).wait()
            arrived(spread.at[c, max(1, g * GROUP) : (g + 1) * GROUP], r2.at[c, g])
            each(1, WA, lambda e, g=g: owner_copy(c, g, e).start())
            owner_keep(c, g).start()

    first_stage(0)

    @pl.when(is_owner)
    def _():
        extra_times_keep().wait()

    def extra_arrived(s):
        @pl.when(slot_source(s) != k)
        def _():
            extra_times_arrival(s).wait_recv()

    each(0, EXTRA_SLOTS, extra_arrived)
    each(1, WA, lambda e: extra_owner_copy(e).start())
    extra_owner_keep().start()

    first_stage(1)
    last_stage(0)
    last_stage(1)

    for m in range(EXTRA):

        @pl.when(owner_of(m) != i)
        def _(m=m):
            extra_copy(m).wait_send()

    for c in range(2):
        arrived(spectra.at[c, :, : WA - 1], s1.at[c])
        arrived(turned.at[c, : KA - 1], s2.at[c])

    @pl.when(is_owner)
    def _():
        arrived(turned.at[2, : KA - 1], s2.at[2])

    arrived(mixed_out, out_sem)
    extra_owner_keep().wait()
    for sem in (s3, r3):
        arrived(own_extra.at[: WA - 1], sem.at[2])
    for c in range(2):
        arrived(own.at[c, 0], local_sem.at[2, c])
        for sem in (s3, r3):
            arrived(own.at[c, : WA - 1], sem.at[c])


def last_kernel(own, own_extra, mixed, coef_in, out, mixed_out, coef_out, times, out_sem):
    k = lax.axis_index("ka")
    z, y = k // 4, k % 4
    passed = pltpu.make_async_copy(mixed, mixed_out, out_sem.at[4])
    passed.start()
    coef_out[...] = coef_in[0, :HIST]

    def place(value, tile):
        value = value.astype(F32)
        times[0, pl.ds(2 * tile, 8)] = value[:8]
        times[1, pl.ds(2 * tile, 8)] = value[8:]

    writes = []
    for row_z in range(4):
        core = row_z % 2

        def row(row_y, _, row_z=row_z, core=core):
            slot = (z - row_z + 4) % 4 * GROUP + (y - row_y + 4) % 4
            first = (4 * row_z + row_y) * TILES
            for c in range(2):
                for n in range(WA):
                    place(own[c, n, slot], first + (c * WA + n) * 4)
            for m in range(EXTRA):
                place(own_extra[2 * ((row_y + m) % 4) + core, row_z // 2 * EXTRA + m], first + EXTRA_START[m])
            return 0

        lax.fori_loop(0, 4, row, 0)
        rows = pl.ds(row_z * GROUP * TILES * 2, GROUP * TILES * 2)
        writes.append(pltpu.make_async_copy(times.at[:, rows], out.at[:, rows], out_sem.at[row_z]))
        writes[-1].start()
    for write in writes:
        write.wait()
    passed.wait()


def shards(sigma_hist, resid_hist, sigma_new, resid_new, slot_order, freq_index, freq_weight):
    vmem = pl.BlockSpec(memory_space=pltpu.VMEM)
    hbm = pl.BlockSpec(memory_space=pltpu.HBM)
    dma = pltpu.SemaphoreType.DMA
    small = (
        jnp.pad(freq_index.astype(F32), (0, 384))
        + jnp.pad(freq_weight, (256, 128))
        + jnp.pad(slot_order.astype(F32), (512, 128 - HIST))
    ).reshape(5, 128)
    own, own_extra, mixed, coeffs = pl.pallas_call(
        main_kernel,
        out_shape=(
            jax.ShapeDtypeStruct((2, WA, KA, 16, 128), BF16),
            jax.ShapeDtypeStruct((WA, EXTRA_SLOTS, 16, 128), BF16),
            jax.ShapeDtypeStruct(sigma_new.shape, BF16),
            jax.ShapeDtypeStruct((8, 128), F32),
        ),
        in_specs=[vmem] + [hbm] * 4,
        out_specs=(hbm, hbm, hbm, vmem),
        scratch_shapes=[
            pltpu.VMEM(sigma_hist.shape, BF16),
            pltpu.VMEM(resid_hist.shape, BF16),
            pltpu.VMEM(sigma_new.shape, BF16),
            pltpu.VMEM(resid_new.shape, BF16),
            pltpu.VMEM((7 * ROWS, 7 * ROWS), F32),
            pltpu.VMEM((HIST + 1, 8, 128), F32),
            pltpu.VMEM((WA, 8, 128), F32),
            pltpu.VMEM((KA, 8, 128), F32),
            pltpu.VMEM((2 * NTAU, 2 * NTAU), BF16),
            pltpu.VMEM((128, 128), BF16),
            pltpu.VMEM((2 * WA + EXTRA, 2, ROWS, UNIT), BF16),
            pltpu.VMEM((3, 2, WA, ROWS, UNIT), BF16),
            pltpu.VMEM((3, KA, WA, 16, 128), BF16),
            pltpu.VMEM((2, KA, WA, 16, 128), BF16),
            pltpu.VMEM((EXTRA_SLOTS, WA, 16, 128), BF16),
            dma((4, 3)),
            dma((4,)),
            dma((2,)),
            dma((3,)),
            dma((EXTRA,)),
            dma((3,)),
            dma((2, GROUPS)),
            dma((EXTRA_SLOTS,)),
            dma((3,)),
            dma((3,)),
            dma,
            dma((3, 3)),
        ],
        compiler_params=pltpu.CompilerParams(
            collective_id=0, has_side_effects=True, vmem_limit_bytes=51 * 2**20
        ),
        name="mix_and_transform",
    )(small, sigma_hist, resid_hist, sigma_new, resid_new)
    out, mixed_sigma, diis_coeffs = pl.pallas_call(
        last_kernel,
        out_shape=(
            jax.ShapeDtypeStruct((2, KA * TILES * 2, 128), F32),
            jax.ShapeDtypeStruct(sigma_new.shape, BF16),
            jax.ShapeDtypeStruct((HIST,), F32),
        ),
        in_specs=[vmem] * 4,
        out_specs=(hbm, hbm, vmem),
        scratch_shapes=[
            pltpu.VMEM((2, KA * TILES * 2, 128), F32),
            dma((5,)),
        ],
        compiler_params=pltpu.CompilerParams(vmem_limit_bytes=16 * 2**20),
        name="unpack",
    )(own, own_extra, mixed, coeffs)
    sigma_tau = out.reshape(2, KA * TILES, 2, 128).transpose(0, 2, 1, 3).reshape(2, 2, KA * WIDTH)
    return (sigma_tau, mixed_sigma, diis_coeffs)


def solution(mesh):
    return jax.shard_map(
        shards,
        mesh=mesh,
        in_specs=(
            P(None, None, "wa", "ka"),
            P(None, None, "wa", "ka"),
            P(None, "wa", "ka"),
            P(None, "wa", "ka"),
            P(),
            P(),
            P(),
        ),
        out_specs=(P(("ka", "wa"), None, None), P(None, "wa", "ka"), P()),
        check_vma=False,
    )
```

```python
import functools
import math

import jax
import jax.numpy as jnp
from jax import lax
from jax.experimental import pallas as pl
from jax.experimental.pallas import tpu as pltpu
from jax.sharding import PartitionSpec as P

MESH = pl.DeviceIdType.MESH
BF16, F32 = jnp.bfloat16, jnp.float32

HIST = 6
NTAU = 256
ROWS = 32
KA, WA = 16, 8
TILES = 75
UNIT = 512
WIDTH = TILES * 128
GRAM_PARTS = ((0, 50), (50, 25))
GRAM_STEP = 25
EXTRA = 3
EXTRA_START = (64, 68, 71)


def sine(x):
    x2 = x * x
    p = -1.0 / 39916800.0
    for factor in (1.0 / 362880.0, -1.0 / 5040.0, 1.0 / 120.0, -1.0 / 6.0, 1.0):
        p = p * x2 + factor
    return x * p


def cosine_of_phase(phase):
    z = 256 - jnp.abs(phase - 512)
    return -sine(z.astype(F32) * (math.pi / 512))


def build_transform(small, table):
    odd_freq = 2 * jnp.concatenate([small[0:1], small[1:2]], axis=1).astype(jnp.int32) + 1
    weight = jnp.concatenate([small[2:3], small[3:4]], axis=1)

    def block(b, _):
        row = b * 64 + lax.broadcasted_iota(jnp.int32, (64, NTAU), 0)
        odd_tau = 2 * (row >> 1) + 1
        part = row & 1
        base = odd_freq * odd_tau + 256 * part
        for other in range(2):
            phase = (base - 256 * other) & 1023
            table[pl.ds(pl.multiple_of(b * 64, 64), 64), other * NTAU : (other + 1) * NTAU] = (
                weight * cosine_of_phase(phase)
            ).astype(BF16)
        return 0

    lax.fori_loop(0, 2 * NTAU // 64, block, 0)


def build_regroup(regroup):
    out = lax.broadcasted_iota(jnp.int32, (128, 128), 0)
    source = ((out >> 1) & 3) * 32 + (out >> 4) * 4 + ((out >> 3) & 1) * 2 + (out & 1)
    here = lax.broadcasted_iota(jnp.int32, (128, 128), 1)
    regroup[...] = jnp.where(source == here, 1.0, 0.0).astype(BF16)


def solve(gram, oldest):
    def entry(s, u):
        return jnp.broadcast_to(gram[s : s + 1, u : u + 1], (8, 128))

    full = {(s, u): entry(s, u) for s in range(HIST + 1) for u in range(s + 1)}
    mat = {}
    for s in range(HIST):
        for u in range(s + 1):
            value = jnp.where(oldest == s, full[HIST, u], full[s, u])
            if s == u:
                value = jnp.where(oldest == s, full[HIST, HIST], full[s, s])
            else:
                value = jnp.where(oldest == u, full[HIST, s], value)
            mat[s, u] = value
    low, inv = {}, {}
    for s in range(HIST):
        for u in range(s + 1):
            value = mat[s, u]
            for w in range(u):
                value = value - low[s, w] * low[u, w]
            if s == u:
                inv[s] = 1.0 / jnp.sqrt(value)
            else:
                low[s, u] = value * inv[u]
    half = {}
    for s in range(HIST):
        value = jnp.ones((8, 128), F32)
        for u in range(s):
            value = value - low[s, u] * half[u]
        half[s] = value * inv[s]
    full_solution = {}
    for s in reversed(range(HIST)):
        value = half[s]
        for u in range(s + 1, HIST):
            value = value - low[u, s] * full_solution[u]
        full_solution[s] = value * inv[s]
    total = full_solution[0]
    for s in range(1, HIST):
        total = total + full_solution[s]
    return [full_solution[s] / total for s in range(HIST)]


def main_kernel(
    small, sig_hist, res_hist, sig_new, res_new,
    own, own_extra, mixed_out, coef_out,
    sig_v, res_v, sign_v, resn_v, acc, weights, gx, gy, table, regroup,
    mixed, spectra, turned,
    in_sem, share_sem, s1, r1, se, s2, r2, out_sem, local_sem,
):
    k, i = lax.axis_index("ka"), lax.axis_index("wa")
    x, core = i // 2, i % 2
    z, y = k // 4, k % 4

    def each(low, high, do):
        def step(d, _):
            do(d)
            return 0

        lax.fori_loop(low, high, step, 0)

    def arrived(ref, sem):
        pltpu.make_async_copy(ref, ref, sem).wait()

    reads = []
    for n, (start, size) in enumerate(GRAM_PARTS):
        cols = pl.ds(start * 128, size * 128)
        reads.append(
            (
                pltpu.make_async_copy(res_hist.at[:, :, :, cols], res_v.at[:, :, :, cols], in_sem.at[0, n]),
                pltpu.make_async_copy(res_new.at[:, :, cols], resn_v.at[:, :, cols], in_sem.at[1, n]),
            )
        )
    sigma_reads = []
    for n, (start, size) in enumerate(((8192, 1408), (0, 4096), (4096, 4096))):
        cols = pl.ds(start, size)
        sigma_reads.append(
            (
                pltpu.make_async_copy(sig_hist.at[:, :, :, cols], sig_v.at[:, :, :, cols], in_sem.at[2, n]),
                pltpu.make_async_copy(sig_new.at[:, :, cols], sign_v.at[:, :, cols], in_sem.at[3, n]),
            )
        )
    for group in reads:
        for read in group:
            read.start()

    barrier = pltpu.get_barrier_semaphore()

    def greet_wa(d, _):
        pl.semaphore_signal(barrier, inc=1, device_id=(k, (i + d) % WA), device_id_type=MESH)
        return 0

    def greet_ka(d, _):
        pl.semaphore_signal(barrier, inc=1, device_id=((k + d) % KA, i), device_id_type=MESH)
        return 0

    lax.fori_loop(1, WA, greet_wa, 0)
    lax.fori_loop(1, KA, greet_ka, 0)

    acc[...] = jnp.zeros_like(acc)
    for n, (start, size) in enumerate(GRAM_PARTS):
        for read in reads[n]:
            read.wait()

        def add_products(b, start=start):
            cols = pl.ds(pl.multiple_of((start + b * GRAM_STEP) * 128, 128), GRAM_STEP * 128)
            total = None
            for ri in range(2):
                block = jnp.concatenate(
                    [res_v[:, ri, :, cols].reshape(HIST * ROWS, GRAM_STEP * 128), resn_v[ri, :, cols]], axis=0
                )
                product = lax.dot_general(block, block, (((1,), (1,)), ((), ())), preferred_element_type=F32)
                total = product if total is None else total + product
            acc[...] += total

        each(0, size // GRAM_STEP, add_products)
    for pair in sigma_reads:
        for read in pair:
            read.start()
    rows = lax.broadcasted_iota(jnp.int32, acc.shape, 0)
    lanes = lax.broadcasted_iota(jnp.int32, acc.shape, 1)
    kept = jnp.where((rows & (ROWS - 1)) == (lanes & (ROWS - 1)), acc[...], 0.0)
    by_lane = jnp.sum(kept.reshape(7, ROWS, 7 * ROWS), axis=1)
    fold = jnp.where(
        lax.broadcasted_iota(jnp.int32, (7 * ROWS, 128), 0) // ROWS
        == lax.broadcasted_iota(jnp.int32, (7 * ROWS, 128), 1),
        1.0,
        0.0,
    )
    share = jnp.dot(by_lane, fold, preferred_element_type=F32, precision=lax.Precision.HIGHEST)
    gx[i] = jnp.concatenate([share, jnp.zeros((1, 128), F32)], axis=0)

    pl.semaphore_wait(barrier, WA - 1 + KA - 1)

    def share_wa(d):
        return pltpu.make_async_remote_copy(
            src_ref=gx.at[i], dst_ref=gx.at[i], send_sem=share_sem.at[0], recv_sem=share_sem.at[1],
            device_id=(k, (i + d) % WA), device_id_type=MESH)

    def share_ka(d):
        return pltpu.make_async_remote_copy(
            src_ref=gy.at[k], dst_ref=gy.at[k], send_sem=share_sem.at[2], recv_sem=share_sem.at[3],
            device_id=((k + d) % KA, i), device_id_type=MESH)

    each(1, WA, lambda d: share_wa(d).start())
    build_transform(small, table)
    build_regroup(regroup)
    for n in range(2):
        arrived(gx.at[: WA - 1], share_sem.at[n])
    total = gx[0]
    for n in range(1, WA):
        total = total + gx[n]
    gy[k] = total
    each(1, KA, lambda d: share_ka(d).start())
    for n in range(2, 4):
        arrived(gy.at[: KA - 1], share_sem.at[n])
    gram = gy[0]
    for n in range(1, KA):
        gram = gram + gy[n]

    oldest = jnp.broadcast_to(small[4:5, 0:1], (8, 128))
    coeffs = solve(gram, oldest)
    lane = lax.broadcasted_iota(jnp.int32, (8, 128), 1)
    packed = jnp.zeros((8, 128), F32)
    newest = jnp.zeros((8, 128), F32)
    for s in range(HIST):
        packed = jnp.where(lane == s, coeffs[s], packed)
        newest = jnp.where(oldest == s, coeffs[s], newest)
        weights[s] = jnp.where(oldest == s, 0.0, coeffs[s])
    weights[HIST] = newest
    coef_out[...] = packed

    def mix(unit, start):
        def rows_of(h, _):
            ri, low = h // 2, pl.multiple_of((h % 2) * 16, 16)
            for tile in range(4):
                cols = pl.ds(pl.multiple_of(start + tile * 128, 128), 128)
                at = (ri, pl.ds(low, 16), cols)
                w = weights[HIST]
                both = jnp.concatenate([w, w], axis=0)
                total = both * (sign_v[at].astype(F32) + resn_v[at].astype(F32))
                for s in range(HIST):
                    w = weights[s]
                    both = jnp.concatenate([w, w], axis=0)
                    total = total + both * (sig_v[(s, *at)].astype(F32) + res_v[(s, *at)].astype(F32))
                mixed[unit, ri, pl.ds(low, 16), tile * 128 : (tile + 1) * 128] = total.astype(BF16)
            return 0

        lax.fori_loop(0, 4, rows_of, 0)

    def unit_copy(c, d):
        j = (i + d) % WA
        return pltpu.make_async_remote_copy(
            src_ref=mixed.at[c * WA + j], dst_ref=spectra.at[c, :, i],
            send_sem=s1.at[c], recv_sem=r1.at[c], device_id=(k, j), device_id_type=MESH)

    def unit_keep(c):
        return pltpu.make_async_copy(mixed.at[c * WA + i], spectra.at[c, :, i], local_sem.at[0, c])

    def owner_of(m):
        return 2 * ((m + y) % 4) + z % 2

    def extra_copy(m):
        return pltpu.make_async_remote_copy(
            src_ref=mixed.at[2 * WA + m], dst_ref=spectra.at[2, :, i],
            send_sem=se.at[m], recv_sem=r1.at[2], device_id=(k, owner_of(m)), device_id_type=MESH)

    def extra_keep(m):
        return pltpu.make_async_copy(mixed.at[2 * WA + m], spectra.at[2, :, i], local_sem.at[0, 2])

    writes = []
    for unit, skip in [(u, 0) for u in range(18)] + [(18, 128)]:
        start = unit * UNIT if unit < 16 else EXTRA_START[unit - 16] * 128
        writes.append(
            pltpu.make_async_copy(
                mixed.at[unit, :, :, skip:UNIT],
                mixed_out.at[:, :, start + skip : start + UNIT],
                out_sem,
            )
        )

    for read in sigma_reads[0]:
        read.wait()
    for m in range(EXTRA):
        mix(2 * WA + m, EXTRA_START[m] * 128)

        @pl.when(owner_of(m) == i)
        def _(m=m):
            extra_keep(m).start()

        @pl.when(owner_of(m) != i)
        def _(m=m):
            extra_copy(m).start()

    for c in range(2):
        for read in sigma_reads[1 + c]:
            read.wait()

        def send_unit(d, c=c):
            unit = c * WA + (i + d) % WA
            mix(unit, unit * UNIT)

            @pl.when(d == 0)
            def _():
                unit_keep(c).start()

            @pl.when(d != 0)
            def _():
                unit_copy(c, d).start()

        each(0, WA, send_unit)
    for write in writes:
        write.start()

    def transform(c):
        def block(b):
            values = jnp.dot(
                table[pl.ds(pl.multiple_of(b * 128, 128), 128)],
                spectra[c].reshape(2 * NTAU, UNIT),
                preferred_element_type=F32,
            ).astype(BF16)
            stacked = jnp.concatenate(
                [
                    jnp.concatenate(
                        [values[n * 32 : (n + 1) * 32, a * 128 : (a + 1) * 128] for a in range(4)], axis=0
                    )
                    for n in range(4)
                ],
                axis=1,
            )
            grouped = jnp.dot(regroup[...], stacked, preferred_element_type=F32).astype(BF16)
            for n in range(4):
                turned[c, pl.ds((4 * b + n) * WA, WA)] = grouped[:, n * 128 : (n + 1) * 128].reshape(WA, 16, 128)

        each(0, 4, block)

    me = k * WA + i
    extra_m = (x - y + 4) % 4
    is_owner = jnp.logical_and(z % 2 == core, extra_m < EXTRA)

    def times_copy(c, n):
        d = KA * WA - n
        pk = (z + d // 32) % 4 * 4 + (y + d // 8 % 4) % 4
        pi = (x + d // 2 % 4) % 4 * 2 + (core + d % 2) % 2
        target = own_extra.at[k * EXTRA + extra_m] if c == 2 else own.at[c, me]
        return pltpu.make_async_remote_copy(
            src_ref=turned.at[c, pk * WA + pi], dst_ref=target,
            send_sem=s2.at[c], recv_sem=r2.at[c], device_id=(pk, pi), device_id_type=MESH)

    def times_keep(c):
        target = own_extra.at[k * EXTRA + extra_m] if c == 2 else own.at[c, me]
        return pltpu.make_async_copy(turned.at[c, me], target, local_sem.at[1, c])

    def send_times(c):
        transform(c)
        each(1, KA * WA, lambda n: times_copy(c, n).start())
        times_keep(c).start()

    @pl.when(is_owner)
    def _():
        extra_keep(0).wait()
        arrived(spectra.at[2, :, : WA - 1], r1.at[2])
        send_times(2)

    for c in range(2):
        unit_keep(c).wait()
        arrived(spectra.at[c, :, : WA - 1], r1.at[c])
        send_times(c)

    for m in range(EXTRA):

        @pl.when(owner_of(m) != i)
        def _(m=m):
            extra_copy(m).wait_send()

    for c in range(2):
        arrived(spectra.at[c, :, : WA - 1], s1.at[c])

    arrived(mixed_out, out_sem)

    @pl.when(is_owner)
    def _():
        times_keep(2).wait()
        arrived(turned.at[2, : KA * WA - 1], s2.at[2])
        arrived(own_extra.at[: KA * EXTRA - 1], r2.at[2])

    @pl.when(jnp.logical_not(is_owner))
    def _():
        arrived(own_extra, r2.at[2])

    for c in range(2):
        times_keep(c).wait()
        arrived(turned.at[c, : KA * WA - 1], s2.at[c])
        arrived(own.at[c, : KA * WA - 1], r2.at[c])


def last_kernel(own, own_extra, mixed, coef_in, out, mixed_out, coef_out, times, out_sem):
    passed = pltpu.make_async_copy(mixed, mixed_out, out_sem.at[4])
    passed.start()
    coef_out[...] = coef_in[0, :HIST]

    def place(value, tile):
        value = value.astype(F32)
        times[0, pl.ds(2 * tile, 8)] = value[:8]
        times[1, pl.ds(2 * tile, 8)] = value[8:]

    writes = []
    for part in range(4):

        def row(n, _, part=part):
            k = 4 * part + n
            for c in range(2):
                for i in range(WA):
                    place(own[c, k * WA + i], k * TILES + (c * WA + i) * 4)
            for m in range(EXTRA):
                place(own_extra[k * EXTRA + m], k * TILES + EXTRA_START[m])
            return 0

        lax.fori_loop(0, 4, row, 0)
        rows = pl.ds(part * 4 * TILES * 2, 4 * TILES * 2)
        writes.append(pltpu.make_async_copy(times.at[:, rows], out.at[:, rows], out_sem.at[part]))
        writes[-1].start()
    for write in writes:
        write.wait()
    passed.wait()


def shards(sigma_hist, resid_hist, sigma_new, resid_new, slot_order, freq_index, freq_weight):
    vmem = pl.BlockSpec(memory_space=pltpu.VMEM)
    hbm = pl.BlockSpec(memory_space=pltpu.HBM)
    dma = pltpu.SemaphoreType.DMA
    small = (
        jnp.pad(freq_index.astype(F32), (0, 384))
        + jnp.pad(freq_weight, (256, 128))
        + jnp.pad(slot_order.astype(F32), (512, 128 - HIST))
    ).reshape(5, 128)
    own, own_extra, mixed, coeffs = pl.pallas_call(
        main_kernel,
        out_shape=(
            jax.ShapeDtypeStruct((2, KA * WA, 16, 128), BF16),
            jax.ShapeDtypeStruct((KA * EXTRA, 16, 128), BF16),
            jax.ShapeDtypeStruct(sigma_new.shape, BF16),
            jax.ShapeDtypeStruct((8, 128), F32),
        ),
        in_specs=[vmem] + [hbm] * 4,
        out_specs=(hbm, hbm, hbm, vmem),
        scratch_shapes=[
            pltpu.VMEM(sigma_hist.shape, BF16),
            pltpu.VMEM(resid_hist.shape, BF16),
            pltpu.VMEM(sigma_new.shape, BF16),
            pltpu.VMEM(resid_new.shape, BF16),
            pltpu.VMEM((7 * ROWS, 7 * ROWS), F32),
            pltpu.VMEM((HIST + 1, 8, 128), F32),
            pltpu.VMEM((WA, 8, 128), F32),
            pltpu.VMEM((KA, 8, 128), F32),
            pltpu.VMEM((2 * NTAU, 2 * NTAU), BF16),
            pltpu.VMEM((128, 128), BF16),
            pltpu.VMEM((2 * WA + EXTRA, 2, ROWS, UNIT), BF16),
            pltpu.VMEM((3, 2, WA, ROWS, UNIT), BF16),
            pltpu.VMEM((3, KA * WA, 16, 128), BF16),
            dma((4, 3)),
            dma((4,)),
            dma((2,)),
            dma((3,)),
            dma((EXTRA,)),
            dma((3,)),
            dma((3,)),
            dma,
            dma((2, 3)),
        ],
        compiler_params=pltpu.CompilerParams(
            collective_id=0, has_side_effects=True, vmem_limit_bytes=51 * 2**20
        ),
        name="mix_and_transform",
    )(small, sigma_hist, resid_hist, sigma_new, resid_new)
    out, mixed_sigma, diis_coeffs = pl.pallas_call(
        last_kernel,
        out_shape=(
            jax.ShapeDtypeStruct((2, KA * TILES * 2, 128), F32),
            jax.ShapeDtypeStruct(sigma_new.shape, BF16),
            jax.ShapeDtypeStruct((HIST,), F32),
        ),
        in_specs=[vmem] * 4,
        out_specs=(hbm, hbm, vmem),
        scratch_shapes=[
            pltpu.VMEM((2, KA * TILES * 2, 128), F32),
            dma((5,)),
        ],
        compiler_params=pltpu.CompilerParams(vmem_limit_bytes=16 * 2**20),
        name="unpack",
    )(own, own_extra, mixed, coeffs)
    sigma_tau = out.reshape(2, KA * TILES, 2, 128).transpose(0, 2, 1, 3).reshape(2, 2, KA * WIDTH)
    return (sigma_tau, mixed_sigma, diis_coeffs)


def solution(mesh):
    return jax.shard_map(
        shards,
        mesh=mesh,
        in_specs=(
            P(None, None, "wa", "ka"),
            P(None, None, "wa", "ka"),
            P(None, "wa", "ka"),
            P(None, "wa", "ka"),
            P(),
            P(),
            P(),
        ),
        out_specs=(P(("ka", "wa"), None, None), P(None, "wa", "ka"), P()),
        check_vma=False,
    )
```

```python
import functools
import math

import jax
import jax.numpy as jnp
from jax import lax
from jax.experimental import pallas as pl
from jax.experimental.pallas import tpu as pltpu
from jax.sharding import PartitionSpec as P

MESH = pl.DeviceIdType.MESH
BF16, F32 = jnp.bfloat16, jnp.float32

HIST = 6
NTAU = 256
ROWS = 32
KA, WA = 16, 8
TILES = 75
UNIT = 512
WIDTH = TILES * 128
GRAM_STEP = 25
GRAM_STEPS = TILES // GRAM_STEP
EXTRA = 3
EXTRA_START = (64, 68, 71)


def sine(x):
    x2 = x * x
    p = -1.0 / 39916800.0
    for factor in (1.0 / 362880.0, -1.0 / 5040.0, 1.0 / 120.0, -1.0 / 6.0, 1.0):
        p = p * x2 + factor
    return x * p


def cosine_of_phase(phase):
    z = 256 - jnp.abs(phase - 512)
    return -sine(z.astype(F32) * (math.pi / 512))


def build_transform(small, weight_ref, table):
    odd_freq = 2 * jnp.concatenate([small[0:1], small[1:2]], axis=1) + 1
    weight = weight_ref[...].reshape(1, NTAU)

    def block(b, _):
        row = b * 64 + lax.broadcasted_iota(jnp.int32, (64, NTAU), 0)
        odd_tau = 2 * (row >> 1) + 1
        part = row & 1
        base = odd_freq * odd_tau + 256 * part
        for other in range(2):
            phase = (base - 256 * other) & 1023
            table[pl.ds(pl.multiple_of(b * 64, 64), 64), other * NTAU : (other + 1) * NTAU] = (
                weight * cosine_of_phase(phase)
            ).astype(BF16)
        return 0

    lax.fori_loop(0, 2 * NTAU // 64, block, 0)


def build_regroup(regroup):
    out = lax.broadcasted_iota(jnp.int32, (128, 128), 0)
    source = ((out >> 1) & 3) * 32 + (out >> 4) * 4 + ((out >> 3) & 1) * 2 + (out & 1)
    here = lax.broadcasted_iota(jnp.int32, (128, 128), 1)
    regroup[...] = jnp.where(source == here, 1.0, 0.0).astype(BF16)


def solve(gram, oldest):
    def entry(s, u):
        return jnp.broadcast_to(gram[s : s + 1, u : u + 1], (8, 128))

    full = {(s, u): entry(s, u) for s in range(HIST + 1) for u in range(s + 1)}
    mat = {}
    for s in range(HIST):
        for u in range(s + 1):
            value = jnp.where(oldest == s, full[HIST, u], full[s, u])
            if s == u:
                value = jnp.where(oldest == s, full[HIST, HIST], full[s, s])
            else:
                value = jnp.where(oldest == u, full[HIST, s], value)
            mat[s, u] = value
    low, inv = {}, {}
    for s in range(HIST):
        for u in range(s + 1):
            value = mat[s, u]
            for w in range(u):
                value = value - low[s, w] * low[u, w]
            if s == u:
                inv[s] = 1.0 / jnp.sqrt(value)
            else:
                low[s, u] = value * inv[u]
    half = {}
    for s in range(HIST):
        value = jnp.ones((8, 128), F32)
        for u in range(s):
            value = value - low[s, u] * half[u]
        half[s] = value * inv[s]
    full_solution = {}
    for s in reversed(range(HIST)):
        value = half[s]
        for u in range(s + 1, HIST):
            value = value - low[u, s] * full_solution[u]
        full_solution[s] = value * inv[s]
    total = full_solution[0]
    for s in range(1, HIST):
        total = total + full_solution[s]
    return [full_solution[s] / total for s in range(HIST)]


def main_kernel(
    small, weight_ref, sig_hist, res_hist, sig_new, res_new,
    own, own_extra, mixed_out, coef_out,
    sig_v, res_v, sign_v, resn_v, acc, weights, gx, gy, table, regroup,
    mixed, spectra, turned,
    in_sem, share_sem, s1, r1, se, s2, r2, out_sem, local_sem,
):
    k, i = lax.axis_index("ka"), lax.axis_index("wa")
    x, core = i // 2, i % 2
    z, y = k // 4, k % 4

    def each(low, high, do):
        def step(d, _):
            do(d)
            return 0

        lax.fori_loop(low, high, step, 0)

    def arrived(ref, sem):
        pltpu.make_async_copy(ref, ref, sem).wait()

    def gram_cols(n):
        return pl.ds(pl.multiple_of(n * (GRAM_STEP * 128), 128), GRAM_STEP * 128)

    def gram_reads(n):
        cols = gram_cols(n)
        return (
            pltpu.make_async_copy(res_hist.at[:, :, :, cols], res_v.at[:, :, :, cols], in_sem.at[0, n]),
            pltpu.make_async_copy(res_new.at[:, :, cols], resn_v.at[:, :, cols], in_sem.at[1, n]),
        )

    sigma_reads = []
    for n, (start, size) in enumerate(((8192, 1408), (0, 4096), (4096, 4096))):
        cols = pl.ds(start, size)
        sigma_reads.append(
            (
                pltpu.make_async_copy(sig_hist.at[:, :, :, cols], sig_v.at[:, :, :, cols], in_sem.at[2, n]),
                pltpu.make_async_copy(sig_new.at[:, :, cols], sign_v.at[:, :, cols], in_sem.at[3, n]),
            )
        )
    for n in range(GRAM_STEPS):
        for read in gram_reads(n):
            read.start()

    barrier = pltpu.get_barrier_semaphore()

    def greet_wa(d, _):
        pl.semaphore_signal(barrier, inc=1, device_id=(k, (i + d) % WA), device_id_type=MESH)
        return 0

    def greet_ka(d, _):
        pl.semaphore_signal(barrier, inc=1, device_id=((k + d) % KA, i), device_id_type=MESH)
        return 0

    lax.fori_loop(1, WA, greet_wa, 0)
    lax.fori_loop(1, KA, greet_ka, 0)

    acc[...] = jnp.zeros_like(acc)

    def add_products(n):
        for read in gram_reads(n):
            read.wait()
        cols = gram_cols(n)
        total = None
        for ri in range(2):
            block = jnp.concatenate(
                [res_v[:, ri, :, cols].reshape(HIST * ROWS, GRAM_STEP * 128), resn_v[ri, :, cols]], axis=0
            )
            product = lax.dot_general(block, block, (((1,), (1,)), ((), ())), preferred_element_type=F32)
            total = product if total is None else total + product
        acc[...] += total

    each(0, GRAM_STEPS, add_products)
    for pair in sigma_reads:
        for read in pair:
            read.start()
    rows = lax.broadcasted_iota(jnp.int32, acc.shape, 0)
    lanes = lax.broadcasted_iota(jnp.int32, acc.shape, 1)
    kept = jnp.where((rows & (ROWS - 1)) == (lanes & (ROWS - 1)), acc[...], 0.0)
    by_lane = jnp.sum(kept.reshape(7, ROWS, 7 * ROWS), axis=1)
    fold = jnp.where(
        lax.broadcasted_iota(jnp.int32, (7 * ROWS, 128), 0) // ROWS
        == lax.broadcasted_iota(jnp.int32, (7 * ROWS, 128), 1),
        1.0,
        0.0,
    )
    share = jnp.dot(by_lane, fold, preferred_element_type=F32, precision=lax.Precision.HIGHEST)
    gx[i] = jnp.concatenate([share, jnp.zeros((1, 128), F32)], axis=0)

    pl.semaphore_wait(barrier, WA - 1 + KA - 1)

    def share_wa(d):
        return pltpu.make_async_remote_copy(
            src_ref=gx.at[i], dst_ref=gx.at[i], send_sem=share_sem.at[0], recv_sem=share_sem.at[1],
            device_id=(k, (i + d) % WA), device_id_type=MESH)

    def share_ka(d):
        return pltpu.make_async_remote_copy(
            src_ref=gy.at[k], dst_ref=gy.at[k], send_sem=share_sem.at[2], recv_sem=share_sem.at[3],
            device_id=((k + d) % KA, i), device_id_type=MESH)

    each(1, WA, lambda d: share_wa(d).start())
    for n in range(2):
        arrived(gx.at[: WA - 1], share_sem.at[n])
    total = gx[0]
    for n in range(1, WA):
        total = total + gx[n]
    gy[k] = total
    each(1, KA, lambda d: share_ka(d).start())
    build_transform(small, weight_ref, table)
    build_regroup(regroup)
    for n in range(2, 4):
        arrived(gy.at[: KA - 1], share_sem.at[n])
    gram = gy[0]
    for n in range(1, KA):
        gram = gram + gy[n]

    oldest = jnp.broadcast_to(small[2:3, 0:1], (8, 128))
    coeffs = solve(gram, oldest)
    lane = lax.broadcasted_iota(jnp.int32, (8, 128), 1)
    packed = jnp.zeros((8, 128), F32)
    newest = jnp.zeros((8, 128), F32)
    for s in range(HIST):
        packed = jnp.where(lane == s, coeffs[s], packed)
        newest = jnp.where(oldest == s, coeffs[s], newest)
        weights[s] = jnp.where(oldest == s, 0.0, coeffs[s])
    weights[HIST] = newest
    coef_out[...] = packed

    def mix(unit, start):
        def rows_of(h, _):
            ri, low = h // 2, pl.multiple_of((h % 2) * 16, 16)
            for tile in range(4):
                cols = pl.ds(pl.multiple_of(start + tile * 128, 128), 128)
                at = (ri, pl.ds(low, 16), cols)
                w = weights[HIST]
                both = jnp.concatenate([w, w], axis=0)
                total = both * (sign_v[at].astype(F32) + resn_v[at].astype(F32))
                for s in range(HIST):
                    w = weights[s]
                    both = jnp.concatenate([w, w], axis=0)
                    total = total + both * (sig_v[(s, *at)].astype(F32) + res_v[(s, *at)].astype(F32))
                mixed[unit, ri, pl.ds(low, 16), tile * 128 : (tile + 1) * 128] = total.astype(BF16)
            return 0

        lax.fori_loop(0, 4, rows_of, 0)

    def unit_copy(c, d):
        j = (i + d) % WA
        return pltpu.make_async_remote_copy(
            src_ref=mixed.at[c * WA + j], dst_ref=spectra.at[c, :, i],
            send_sem=s1.at[c], recv_sem=r1.at[c], device_id=(k, j), device_id_type=MESH)

    def unit_keep(c):
        return pltpu.make_async_copy(mixed.at[c * WA + i], spectra.at[c, :, i], local_sem.at[0, c])

    def owner_of(m):
        return 2 * ((m + y) % 4) + z % 2

    def extra_copy(m):
        return pltpu.make_async_remote_copy(
            src_ref=mixed.at[2 * WA + m], dst_ref=spectra.at[2, :, i],
            send_sem=se.at[m], recv_sem=r1.at[2], device_id=(k, owner_of(m)), device_id_type=MESH)

    def extra_keep(m):
        return pltpu.make_async_copy(mixed.at[2 * WA + m], spectra.at[2, :, i], local_sem.at[0, 2])

    writes = []
    for unit, skip in [(u, 0) for u in range(18)] + [(18, 128)]:
        start = unit * UNIT if unit < 16 else EXTRA_START[unit - 16] * 128
        writes.append(
            pltpu.make_async_copy(
                mixed.at[unit, :, :, skip:UNIT],
                mixed_out.at[:, :, start + skip : start + UNIT],
                out_sem,
            )
        )

    for read in sigma_reads[0]:
        read.wait()
    for m in range(EXTRA):
        mix(2 * WA + m, EXTRA_START[m] * 128)

        @pl.when(owner_of(m) == i)
        def _(m=m):
            extra_keep(m).start()

        @pl.when(owner_of(m) != i)
        def _(m=m):
            extra_copy(m).start()

    for c in range(2):
        for read in sigma_reads[1 + c]:
            read.wait()

        def send_unit(d, c=c):
            unit = c * WA + (i + d) % WA
            mix(unit, unit * UNIT)

            @pl.when(d == WA)
            def _():
                unit_keep(c).start()

            @pl.when(d != WA)
            def _():
                unit_copy(c, d).start()

        each(1, WA + 1, send_unit)
    for write in writes:
        write.start()

    def transform(c):
        def block(b):
            values = jnp.dot(
                table[pl.ds(pl.multiple_of(b * 128, 128), 128)],
                spectra[c].reshape(2 * NTAU, UNIT),
                preferred_element_type=F32,
            ).astype(BF16)
            stacked = jnp.concatenate(
                [
                    jnp.concatenate(
                        [values[n * 32 : (n + 1) * 32, a * 128 : (a + 1) * 128] for a in range(4)], axis=0
                    )
                    for n in range(4)
                ],
                axis=1,
            )
            grouped = jnp.dot(regroup[...], stacked, preferred_element_type=F32).astype(BF16)
            for n in range(4):
                turned[c, pl.ds((4 * b + n) * WA, WA)] = grouped[:, n * 128 : (n + 1) * 128].reshape(WA, 16, 128)

        each(0, 4, block)

    me = k * WA + i
    extra_m = (x - y + 4) % 4
    is_owner = jnp.logical_and(z % 2 == core, extra_m < EXTRA)

    def times_copy(c, n):
        d = KA * WA - n
        pk = (z + d // 32) % 4 * 4 + (y + d // 8 % 4) % 4
        pi = (x + d // 2 % 4) % 4 * 2 + (core + d % 2) % 2
        target = own_extra.at[k * EXTRA + extra_m] if c == 2 else own.at[c, me]
        return pltpu.make_async_remote_copy(
            src_ref=turned.at[c, pk * WA + pi], dst_ref=target,
            send_sem=s2.at[c], recv_sem=r2.at[c], device_id=(pk, pi), device_id_type=MESH)

    def times_keep(c):
        target = own_extra.at[k * EXTRA + extra_m] if c == 2 else own.at[c, me]
        return pltpu.make_async_copy(turned.at[c, me], target, local_sem.at[1, c])

    def send_times(c):
        transform(c)
        each(1, KA * WA, lambda n: times_copy(c, n).start())
        times_keep(c).start()

    @pl.when(is_owner)
    def _():
        extra_keep(0).wait()
        arrived(spectra.at[2, :, : WA - 1], r1.at[2])
        send_times(2)

    for c in range(2):
        unit_keep(c).wait()
        arrived(spectra.at[c, :, : WA - 1], r1.at[c])
        send_times(c)

    for m in range(EXTRA):

        @pl.when(owner_of(m) != i)
        def _(m=m):
            extra_copy(m).wait_send()

    for c in range(2):
        arrived(spectra.at[c, :, : WA - 1], s1.at[c])

    arrived(mixed_out, out_sem)

    @pl.when(is_owner)
    def _():
        times_keep(2).wait()
        arrived(turned.at[2, : KA * WA - 1], s2.at[2])
        arrived(own_extra.at[: KA * EXTRA - 1], r2.at[2])

    @pl.when(jnp.logical_not(is_owner))
    def _():
        arrived(own_extra, r2.at[2])

    for c in range(2):
        times_keep(c).wait()
        arrived(turned.at[c, : KA * WA - 1], s2.at[c])
        arrived(own.at[c, : KA * WA - 1], r2.at[c])


def last_kernel(own, own_extra, mixed, coef_in, out, mixed_out, coef_out, times, out_sem):
    passed = pltpu.make_async_copy(mixed, mixed_out, out_sem.at[4])
    passed.start()
    coef_out[...] = coef_in[0, :HIST]

    def place(value, tile):
        value = value.astype(F32)
        times[0, pl.ds(2 * tile, 8)] = value[:8]
        times[1, pl.ds(2 * tile, 8)] = value[8:]

    writes = []
    for part in range(4):

        def row(n, _, part=part):
            k = 4 * part + n
            for c in range(2):
                for i in range(WA):
                    place(own[c, k * WA + i], k * TILES + (c * WA + i) * 4)
            for m in range(EXTRA):
                place(own_extra[k * EXTRA + m], k * TILES + EXTRA_START[m])
            return 0

        lax.fori_loop(0, 4, row, 0)
        rows = pl.ds(part * 4 * TILES * 2, 4 * TILES * 2)
        writes.append(pltpu.make_async_copy(times.at[:, rows], out.at[:, rows], out_sem.at[part]))
        writes[-1].start()
    for write in writes:
        write.wait()
    passed.wait()


def shards(sigma_hist, resid_hist, sigma_new, resid_new, slot_order, freq_index, freq_weight):
    vmem = pl.BlockSpec(memory_space=pltpu.VMEM)
    hbm = pl.BlockSpec(memory_space=pltpu.HBM)
    dma = pltpu.SemaphoreType.DMA
    small = (jnp.pad(freq_index, (0, 128)) + jnp.pad(slot_order, (NTAU, 128 - HIST))).reshape(3, 128)
    own, own_extra, mixed, coeffs = pl.pallas_call(
        main_kernel,
        out_shape=(
            jax.ShapeDtypeStruct((2, KA * WA, 16, 128), BF16),
            jax.ShapeDtypeStruct((KA * EXTRA, 16, 128), BF16),
            jax.ShapeDtypeStruct(sigma_new.shape, BF16),
            jax.ShapeDtypeStruct((8, 128), F32),
        ),
        in_specs=[vmem] * 2 + [hbm] * 4,
        out_specs=(hbm, hbm, hbm, vmem),
        scratch_shapes=[
            pltpu.VMEM(sigma_hist.shape, BF16),
            pltpu.VMEM(resid_hist.shape, BF16),
            pltpu.VMEM(sigma_new.shape, BF16),
            pltpu.VMEM(resid_new.shape, BF16),
            pltpu.VMEM((7 * ROWS, 7 * ROWS), F32),
            pltpu.VMEM((HIST + 1, 8, 128), F32),
            pltpu.VMEM((WA, 8, 128), F32),
            pltpu.VMEM((KA, 8, 128), F32),
            pltpu.VMEM((2 * NTAU, 2 * NTAU), BF16),
            pltpu.VMEM((128, 128), BF16),
            pltpu.VMEM((2 * WA + EXTRA, 2, ROWS, UNIT), BF16),
            pltpu.VMEM((3, 2, WA, ROWS, UNIT), BF16),
            pltpu.VMEM((3, KA * WA, 16, 128), BF16),
            dma((4, 3)),
            dma((4,)),
            dma((2,)),
            dma((3,)),
            dma((EXTRA,)),
            dma((3,)),
            dma((3,)),
            dma,
            dma((2, 3)),
        ],
        compiler_params=pltpu.CompilerParams(
            collective_id=0, has_side_effects=True, vmem_limit_bytes=51 * 2**20
        ),
        name="mix_and_transform",
    )(small, freq_weight, sigma_hist, resid_hist, sigma_new, resid_new)
    out, mixed_sigma, diis_coeffs = pl.pallas_call(
        last_kernel,
        out_shape=(
            jax.ShapeDtypeStruct((2, KA * TILES * 2, 128), F32),
            jax.ShapeDtypeStruct(sigma_new.shape, BF16),
            jax.ShapeDtypeStruct((HIST,), F32),
        ),
        in_specs=[vmem] * 4,
        out_specs=(hbm, hbm, vmem),
        scratch_shapes=[
            pltpu.VMEM((2, KA * TILES * 2, 128), F32),
            dma((5,)),
        ],
        compiler_params=pltpu.CompilerParams(vmem_limit_bytes=16 * 2**20),
        name="unpack",
    )(own, own_extra, mixed, coeffs)
    sigma_tau = out.reshape(2, KA * TILES, 2, 128).transpose(0, 2, 1, 3).reshape(2, 2, KA * WIDTH)
    return (sigma_tau, mixed_sigma, diis_coeffs)


def solution(mesh):
    return jax.shard_map(
        shards,
        mesh=mesh,
        in_specs=(
            P(None, None, "wa", "ka"),
            P(None, None, "wa", "ka"),
            P(None, "wa", "ka"),
            P(None, "wa", "ka"),
            P(),
            P(),
            P(),
        ),
        out_specs=(P(("ka", "wa"), None, None), P(None, "wa", "ka"), P()),
        check_vma=False,
    )
```

```python
import functools
import math

import jax
import jax.numpy as jnp
from jax import lax
from jax.experimental import pallas as pl
from jax.experimental.pallas import tpu as pltpu
from jax.sharding import PartitionSpec as P

MESH = pl.DeviceIdType.MESH
BF16, F32 = jnp.bfloat16, jnp.float32

HIST = 6
NTAU = 256
ROWS = 32
KA, WA = 16, 8
TILES = 75
UNIT = 512
WIDTH = TILES * 128
GRAM_STEP = 25
GRAM_STEPS = TILES // GRAM_STEP
EXTRA = 3
EXTRA_START = (64, 68, 71)


def sine(x):
    x2 = x * x
    p = -1.0 / 39916800.0
    for factor in (1.0 / 362880.0, -1.0 / 5040.0, 1.0 / 120.0, -1.0 / 6.0, 1.0):
        p = p * x2 + factor
    return x * p


def cosine_of_phase(phase):
    z = 256 - jnp.abs(phase - 512)
    return -sine(z.astype(F32) * (math.pi / 512))


def build_transform(small, table):
    odd_freq = 2 * jnp.concatenate([small[0:1], small[1:2]], axis=1).astype(jnp.int32) + 1
    weight = jnp.concatenate([small[2:3], small[3:4]], axis=1)

    def block(b, _):
        row = b * 64 + lax.broadcasted_iota(jnp.int32, (64, NTAU), 0)
        odd_tau = 2 * (row >> 1) + 1
        part = row & 1
        base = odd_freq * odd_tau + 256 * part
        for other in range(2):
            phase = (base - 256 * other) & 1023
            table[pl.ds(pl.multiple_of(b * 64, 64), 64), other * NTAU : (other + 1) * NTAU] = (
                weight * cosine_of_phase(phase)
            ).astype(BF16)
        return 0

    lax.fori_loop(0, 2 * NTAU // 64, block, 0)


def build_regroup(regroup):
    out = lax.broadcasted_iota(jnp.int32, (128, 128), 0)
    source = ((out >> 1) & 3) * 32 + (out >> 4) * 4 + ((out >> 3) & 1) * 2 + (out & 1)
    here = lax.broadcasted_iota(jnp.int32, (128, 128), 1)
    regroup[...] = jnp.where(source == here, 1.0, 0.0).astype(BF16)


def solve(gram, oldest):
    def entry(s, u):
        return jnp.broadcast_to(gram[s : s + 1, u : u + 1], (8, 128))

    full = {(s, u): entry(s, u) for s in range(HIST + 1) for u in range(s + 1)}
    mat = {}
    for s in range(HIST):
        for u in range(s + 1):
            value = jnp.where(oldest == s, full[HIST, u], full[s, u])
            if s == u:
                value = jnp.where(oldest == s, full[HIST, HIST], full[s, s])
            else:
                value = jnp.where(oldest == u, full[HIST, s], value)
            mat[s, u] = value
    low, inv = {}, {}
    for s in range(HIST):
        for u in range(s + 1):
            value = mat[s, u]
            for w in range(u):
                value = value - low[s, w] * low[u, w]
            if s == u:
                inv[s] = 1.0 / jnp.sqrt(value)
            else:
                low[s, u] = value * inv[u]
    half = {}
    for s in range(HIST):
        value = jnp.ones((8, 128), F32)
        for u in range(s):
            value = value - low[s, u] * half[u]
        half[s] = value * inv[s]
    full_solution = {}
    for s in reversed(range(HIST)):
        value = half[s]
        for u in range(s + 1, HIST):
            value = value - low[u, s] * full_solution[u]
        full_solution[s] = value * inv[s]
    total = full_solution[0]
    for s in range(1, HIST):
        total = total + full_solution[s]
    return [full_solution[s] / total for s in range(HIST)]


def main_kernel(
    small, sig_hist, res_hist, sig_new, res_new,
    own, own_extra, mixed_out, coef_out,
    sig_v, res_v, sign_v, resn_v, acc, weights, gx, gy, table, regroup,
    mixed, spectra, turned,
    in_sem, share_sem, s1, r1, se, s2, r2, out_sem, local_sem,
):
    k, i = lax.axis_index("ka"), lax.axis_index("wa")
    x, core = i // 2, i % 2
    z, y = k // 4, k % 4

    def each(low, high, do):
        def step(d, _):
            do(d)
            return 0

        lax.fori_loop(low, high, step, 0)

    def arrived(ref, sem):
        pltpu.make_async_copy(ref, ref, sem).wait()

    def gram_cols(n):
        return pl.ds(pl.multiple_of(n * (GRAM_STEP * 128), 128), GRAM_STEP * 128)

    def gram_reads(n):
        cols = gram_cols(n)
        return (
            pltpu.make_async_copy(res_hist.at[:, :, :, cols], res_v.at[:, :, :, cols], in_sem.at[0, n]),
            pltpu.make_async_copy(res_new.at[:, :, cols], resn_v.at[:, :, cols], in_sem.at[1, n]),
        )

    sigma_reads = []
    for n, (start, size) in enumerate(((8192, 1408), (0, 4096), (4096, 4096))):
        cols = pl.ds(start, size)
        sigma_reads.append(
            (
                pltpu.make_async_copy(sig_hist.at[:, :, :, cols], sig_v.at[:, :, :, cols], in_sem.at[2, n]),
                pltpu.make_async_copy(sig_new.at[:, :, cols], sign_v.at[:, :, cols], in_sem.at[3, n]),
            )
        )
    for n in range(GRAM_STEPS):
        for read in gram_reads(n):
            read.start()

    barrier = pltpu.get_barrier_semaphore()

    def greet_wa(d, _):
        pl.semaphore_signal(barrier, inc=1, device_id=(k, (i + d) % WA), device_id_type=MESH)
        return 0

    def greet_ka(d, _):
        pl.semaphore_signal(barrier, inc=1, device_id=((k + d) % KA, i), device_id_type=MESH)
        return 0

    lax.fori_loop(1, WA, greet_wa, 0)
    lax.fori_loop(1, KA, greet_ka, 0)

    acc[...] = jnp.zeros_like(acc)

    def add_products(n):
        for read in gram_reads(n):
            read.wait()
        cols = gram_cols(n)
        total = None
        for ri in range(2):
            block = jnp.concatenate(
                [res_v[:, ri, :, cols].reshape(HIST * ROWS, GRAM_STEP * 128), resn_v[ri, :, cols]], axis=0
            )
            product = lax.dot_general(block, block, (((1,), (1,)), ((), ())), preferred_element_type=F32)
            total = product if total is None else total + product
        acc[...] += total

    each(0, GRAM_STEPS, add_products)
    for pair in sigma_reads:
        for read in pair:
            read.start()
    rows = lax.broadcasted_iota(jnp.int32, acc.shape, 0)
    lanes = lax.broadcasted_iota(jnp.int32, acc.shape, 1)
    kept = jnp.where((rows & (ROWS - 1)) == (lanes & (ROWS - 1)), acc[...], 0.0)
    by_lane = jnp.sum(kept.reshape(7, ROWS, 7 * ROWS), axis=1)
    fold = jnp.where(
        lax.broadcasted_iota(jnp.int32, (7 * ROWS, 128), 0) // ROWS
        == lax.broadcasted_iota(jnp.int32, (7 * ROWS, 128), 1),
        1.0,
        0.0,
    )
    share = jnp.dot(by_lane, fold, preferred_element_type=F32, precision=lax.Precision.HIGHEST)
    gx[i] = jnp.concatenate([share, jnp.zeros((1, 128), F32)], axis=0)

    pl.semaphore_wait(barrier, WA - 1 + KA - 1)

    def share_wa(d):
        return pltpu.make_async_remote_copy(
            src_ref=gx.at[i], dst_ref=gx.at[i], send_sem=share_sem.at[0], recv_sem=share_sem.at[1],
            device_id=(k, (i + d) % WA), device_id_type=MESH)

    def share_ka(d):
        return pltpu.make_async_remote_copy(
            src_ref=gy.at[k], dst_ref=gy.at[k], send_sem=share_sem.at[2], recv_sem=share_sem.at[3],
            device_id=((k + d) % KA, i), device_id_type=MESH)

    each(1, WA, lambda d: share_wa(d).start())
    for n in range(2):
        arrived(gx.at[: WA - 1], share_sem.at[n])
    total = gx[0]
    for n in range(1, WA):
        total = total + gx[n]
    gy[k] = total
    each(1, KA, lambda d: share_ka(d).start())
    build_transform(small, table)
    build_regroup(regroup)
    for n in range(2, 4):
        arrived(gy.at[: KA - 1], share_sem.at[n])
    gram = gy[0]
    for n in range(1, KA):
        gram = gram + gy[n]

    oldest = jnp.broadcast_to(small[4:5, 0:1], (8, 128))
    coeffs = solve(gram, oldest)
    lane = lax.broadcasted_iota(jnp.int32, (8, 128), 1)
    packed = jnp.zeros((8, 128), F32)
    newest = jnp.zeros((8, 128), F32)
    for s in range(HIST):
        packed = jnp.where(lane == s, coeffs[s], packed)
        newest = jnp.where(oldest == s, coeffs[s], newest)
        weights[s] = jnp.where(oldest == s, 0.0, coeffs[s])
    weights[HIST] = newest
    coef_out[...] = packed

    def mix(unit, start):
        def rows_of(h, _):
            ri, low = h // 2, pl.multiple_of((h % 2) * 16, 16)
            for tile in range(4):
                cols = pl.ds(pl.multiple_of(start + tile * 128, 128), 128)
                at = (ri, pl.ds(low, 16), cols)
                w = weights[HIST]
                both = jnp.concatenate([w, w], axis=0)
                total = both * (sign_v[at].astype(F32) + resn_v[at].astype(F32))
                for s in range(HIST):
                    w = weights[s]
                    both = jnp.concatenate([w, w], axis=0)
                    total = total + both * (sig_v[(s, *at)].astype(F32) + res_v[(s, *at)].astype(F32))
                mixed[unit, ri, pl.ds(low, 16), tile * 128 : (tile + 1) * 128] = total.astype(BF16)
            return 0

        lax.fori_loop(0, 4, rows_of, 0)

    def unit_copy(c, d):
        j = (i + d) % WA
        return pltpu.make_async_remote_copy(
            src_ref=mixed.at[c * WA + j], dst_ref=spectra.at[c, :, i],
            send_sem=s1.at[c], recv_sem=r1.at[c], device_id=(k, j), device_id_type=MESH)

    def unit_keep(c):
        return pltpu.make_async_copy(mixed.at[c * WA + i], spectra.at[c, :, i], local_sem.at[0, c])

    def owner_of(m):
        return 2 * ((m + y) % 4) + z % 2

    def extra_copy(m):
        return pltpu.make_async_remote_copy(
            src_ref=mixed.at[2 * WA + m], dst_ref=spectra.at[2, :, i],
            send_sem=se.at[m], recv_sem=r1.at[2], device_id=(k, owner_of(m)), device_id_type=MESH)

    def extra_keep(m):
        return pltpu.make_async_copy(mixed.at[2 * WA + m], spectra.at[2, :, i], local_sem.at[0, 2])

    writes = []
    for unit, skip in [(u, 0) for u in range(18)] + [(18, 128)]:
        start = unit * UNIT if unit < 16 else EXTRA_START[unit - 16] * 128
        writes.append(
            pltpu.make_async_copy(
                mixed.at[unit, :, :, skip:UNIT],
                mixed_out.at[:, :, start + skip : start + UNIT],
                out_sem,
            )
        )

    for read in sigma_reads[0]:
        read.wait()
    for m in range(EXTRA):
        mix(2 * WA + m, EXTRA_START[m] * 128)

        @pl.when(owner_of(m) == i)
        def _(m=m):
            extra_keep(m).start()

        @pl.when(owner_of(m) != i)
        def _(m=m):
            extra_copy(m).start()

    for c in range(2):
        for read in sigma_reads[1 + c]:
            read.wait()

        def send_unit(d, c=c):
            unit = c * WA + (i + d) % WA
            mix(unit, unit * UNIT)

            @pl.when(d == WA)
            def _():
                unit_keep(c).start()

            @pl.when(d != WA)
            def _():
                unit_copy(c, d).start()

        each(1, WA + 1, send_unit)
    for write in writes:
        write.start()

    def transform(c, b):
        values = jnp.dot(
            table[pl.ds(pl.multiple_of(b * 128, 128), 128)],
            spectra[c].reshape(2 * NTAU, UNIT),
            preferred_element_type=F32,
        ).astype(BF16)
        stacked = jnp.concatenate(
            [
                jnp.concatenate(
                    [values[n * 32 : (n + 1) * 32, a * 128 : (a + 1) * 128] for a in range(4)], axis=0
                )
                for n in range(4)
            ],
            axis=1,
        )
        grouped = jnp.dot(regroup[...], stacked, preferred_element_type=F32).astype(BF16)
        for n in range(4):
            turned[c, pl.ds((4 * b + n) * WA, WA)] = grouped[:, n * 128 : (n + 1) * 128].reshape(WA, 16, 128)

    me = k * WA + i
    extra_m = (x - y + 4) % 4
    is_owner = jnp.logical_and(z % 2 == core, extra_m < EXTRA)

    def times_copy(c, n):
        d = KA * WA - 1 - n
        pk = (z + d // 32) % 4 * 4 + (y + d // 8 % 4) % 4
        pi = (x + d // 2 % 4) % 4 * 2 + (core + d % 2) % 2
        target = own_extra.at[k * EXTRA + extra_m] if c == 2 else own.at[c, me]
        return pltpu.make_async_remote_copy(
            src_ref=turned.at[c, pk * WA + pi], dst_ref=target,
            send_sem=s2.at[c], recv_sem=r2.at[c], device_id=(pk, pi), device_id_type=MESH)

    def times_keep(c):
        target = own_extra.at[k * EXTRA + extra_m] if c == 2 else own.at[c, me]
        return pltpu.make_async_copy(turned.at[c, me], target, local_sem.at[1, c])

    def send_times(c):
        def to_z(q):
            transform(c, (z + 3 - q) % 4)
            each(32 * q, 32 * (q + 1) - q // 3, lambda n: times_copy(c, n).start())

        each(0, 4, to_z)
        times_keep(c).start()

    @pl.when(is_owner)
    def _():
        extra_keep(0).wait()
        arrived(spectra.at[2, :, : WA - 1], r1.at[2])
        send_times(2)

    for c in range(2):
        unit_keep(c).wait()
        arrived(spectra.at[c, :, : WA - 1], r1.at[c])
        send_times(c)

    for m in range(EXTRA):

        @pl.when(owner_of(m) != i)
        def _(m=m):
            extra_copy(m).wait_send()

    for c in range(2):
        arrived(spectra.at[c, :, : WA - 1], s1.at[c])

    arrived(mixed_out, out_sem)

    @pl.when(is_owner)
    def _():
        times_keep(2).wait()
        arrived(turned.at[2, : KA * WA - 1], s2.at[2])
        arrived(own_extra.at[: KA * EXTRA - 1], r2.at[2])

    @pl.when(jnp.logical_not(is_owner))
    def _():
        arrived(own_extra, r2.at[2])

    for c in range(2):
        times_keep(c).wait()
        arrived(turned.at[c, : KA * WA - 1], s2.at[c])
        arrived(own.at[c, : KA * WA - 1], r2.at[c])


def last_kernel(own, own_extra, mixed, coef_in, out, mixed_out, coef_out, times, out_sem):
    passed = pltpu.make_async_copy(mixed, mixed_out, out_sem.at[4])
    passed.start()
    coef_out[...] = coef_in[0, :HIST]

    def place(value, tile):
        value = value.astype(F32)
        times[0, pl.ds(2 * tile, 8)] = value[:8]
        times[1, pl.ds(2 * tile, 8)] = value[8:]

    writes = []
    for part in range(4):

        def row(n, _, part=part):
            k = 4 * part + n
            for c in range(2):
                for i in range(WA):
                    place(own[c, k * WA + i], k * TILES + (c * WA + i) * 4)
            for m in range(EXTRA):
                place(own_extra[k * EXTRA + m], k * TILES + EXTRA_START[m])
            return 0

        lax.fori_loop(0, 4, row, 0)
        rows = pl.ds(part * 4 * TILES * 2, 4 * TILES * 2)
        writes.append(pltpu.make_async_copy(times.at[:, rows], out.at[:, rows], out_sem.at[part]))
        writes[-1].start()
    for write in writes:
        write.wait()
    passed.wait()


def shards(sigma_hist, resid_hist, sigma_new, resid_new, slot_order, freq_index, freq_weight):
    vmem = pl.BlockSpec(memory_space=pltpu.VMEM)
    hbm = pl.BlockSpec(memory_space=pltpu.HBM)
    dma = pltpu.SemaphoreType.DMA
    whole = jnp.pad(freq_index, (0, 384)) + jnp.pad(slot_order, (2 * NTAU, 128 - HIST))
    small = (whole.astype(F32) + jnp.pad(freq_weight, (NTAU, 128))).reshape(5, 128)
    own, own_extra, mixed, coeffs = pl.pallas_call(
        main_kernel,
        out_shape=(
            jax.ShapeDtypeStruct((2, KA * WA, 16, 128), BF16),
            jax.ShapeDtypeStruct((KA * EXTRA, 16, 128), BF16),
            jax.ShapeDtypeStruct(sigma_new.shape, BF16),
            jax.ShapeDtypeStruct((8, 128), F32),
        ),
        in_specs=[vmem] + [hbm] * 4,
        out_specs=(hbm, hbm, hbm, vmem),
        scratch_shapes=[
            pltpu.VMEM(sigma_hist.shape, BF16),
            pltpu.VMEM(resid_hist.shape, BF16),
            pltpu.VMEM(sigma_new.shape, BF16),
            pltpu.VMEM(resid_new.shape, BF16),
            pltpu.VMEM((7 * ROWS, 7 * ROWS), F32),
            pltpu.VMEM((HIST + 1, 8, 128), F32),
            pltpu.VMEM((WA, 8, 128), F32),
            pltpu.VMEM((KA, 8, 128), F32),
            pltpu.VMEM((2 * NTAU, 2 * NTAU), BF16),
            pltpu.VMEM((128, 128), BF16),
            pltpu.VMEM((2 * WA + EXTRA, 2, ROWS, UNIT), BF16),
            pltpu.VMEM((3, 2, WA, ROWS, UNIT), BF16),
            pltpu.VMEM((3, KA * WA, 16, 128), BF16),
            dma((4, 3)),
            dma((4,)),
            dma((2,)),
            dma((3,)),
            dma((EXTRA,)),
            dma((3,)),
            dma((3,)),
            dma,
            dma((2, 3)),
        ],
        compiler_params=pltpu.CompilerParams(
            collective_id=0, has_side_effects=True, vmem_limit_bytes=51 * 2**20
        ),
        name="mix_and_transform",
    )(small, sigma_hist, resid_hist, sigma_new, resid_new)
    out, mixed_sigma, diis_coeffs = pl.pallas_call(
        last_kernel,
        out_shape=(
            jax.ShapeDtypeStruct((2, KA * TILES * 2, 128), F32),
            jax.ShapeDtypeStruct(sigma_new.shape, BF16),
            jax.ShapeDtypeStruct((HIST,), F32),
        ),
        in_specs=[vmem] * 4,
        out_specs=(hbm, hbm, vmem),
        scratch_shapes=[
            pltpu.VMEM((2, KA * TILES * 2, 128), F32),
            dma((5,)),
        ],
        compiler_params=pltpu.CompilerParams(vmem_limit_bytes=16 * 2**20),
        name="unpack",
    )(own, own_extra, mixed, coeffs)
    sigma_tau = out.reshape(2, KA * TILES, 2, 128).transpose(0, 2, 1, 3).reshape(2, 2, KA * WIDTH)
    return (sigma_tau, mixed_sigma, diis_coeffs)


def solution(mesh):
    return jax.shard_map(
        shards,
        mesh=mesh,
        in_specs=(
            P(None, None, "wa", "ka"),
            P(None, None, "wa", "ka"),
            P(None, "wa", "ka"),
            P(None, "wa", "ka"),
            P(),
            P(),
            P(),
        ),
        out_specs=(P(("ka", "wa"), None, None), P(None, "wa", "ka"), P()),
        check_vma=False,
    )
```

```python
import functools
import math

import jax
import jax.numpy as jnp
from jax import lax
from jax.experimental import pallas as pl
from jax.experimental.pallas import tpu as pltpu
from jax.sharding import PartitionSpec as P

MESH = pl.DeviceIdType.MESH
BF16, F32 = jnp.bfloat16, jnp.float32

HIST = 6
NTAU = 256
ROWS = 32
KA, WA = 16, 8
TILES = 75
UNIT = 512
WIDTH = TILES * 128
GRAM_STEP = 25
GRAM_STEPS = TILES // GRAM_STEP
EXTRA = 3
EXTRA_START = (64, 68, 71)


def sine(x):
    x2 = x * x
    p = -1.0 / 39916800.0
    for factor in (1.0 / 362880.0, -1.0 / 5040.0, 1.0 / 120.0, -1.0 / 6.0, 1.0):
        p = p * x2 + factor
    return x * p


def cosine_of_phase(phase):
    z = 256 - jnp.abs(phase - 512)
    return -sine(z.astype(F32) * (math.pi / 512))


def build_transform(small, table):
    odd_freq = 2 * jnp.concatenate([small[0:1], small[1:2]], axis=1).astype(jnp.int32) + 1
    weight = jnp.concatenate([small[2:3], small[3:4]], axis=1)

    def block(b, _):
        row = b * 64 + lax.broadcasted_iota(jnp.int32, (64, NTAU), 0)
        odd_tau = 2 * (row >> 1) + 1
        part = row & 1
        base = odd_freq * odd_tau + 256 * part
        for other in range(2):
            phase = (base - 256 * other) & 1023
            table[pl.ds(pl.multiple_of(b * 64, 64), 64), other * NTAU : (other + 1) * NTAU] = (
                weight * cosine_of_phase(phase)
            ).astype(BF16)
        return 0

    lax.fori_loop(0, 2 * NTAU // 64, block, 0)


def build_regroup(regroup):
    out = lax.broadcasted_iota(jnp.int32, (128, 128), 0)
    source = ((out >> 1) & 3) * 32 + (out >> 4) * 4 + ((out >> 3) & 1) * 2 + (out & 1)
    here = lax.broadcasted_iota(jnp.int32, (128, 128), 1)
    regroup[...] = jnp.where(source == here, 1.0, 0.0).astype(BF16)


def solve(gram, oldest):
    def entry(s, u):
        return jnp.broadcast_to(gram[:, 16 * s + u : 16 * s + u + 1], (8, 128))

    full = {(s, u): entry(s, u) for s in range(HIST + 1) for u in range(s + 1)}
    mat = {}
    for s in range(HIST):
        for u in range(s + 1):
            value = jnp.where(oldest == s, full[HIST, u], full[s, u])
            if s == u:
                value = jnp.where(oldest == s, full[HIST, HIST], full[s, s])
            else:
                value = jnp.where(oldest == u, full[HIST, s], value)
            mat[s, u] = value
    low, inv = {}, {}
    for s in range(HIST):
        for u in range(s + 1):
            value = mat[s, u]
            for w in range(u):
                value = value - low[s, w] * low[u, w]
            if s == u:
                inv[s] = 1.0 / jnp.sqrt(value)
            else:
                low[s, u] = value * inv[u]
    half = {}
    for s in range(HIST):
        value = jnp.ones((8, 128), F32)
        for u in range(s):
            value = value - low[s, u] * half[u]
        half[s] = value * inv[s]
    full_solution = {}
    for s in reversed(range(HIST)):
        value = half[s]
        for u in range(s + 1, HIST):
            value = value - low[u, s] * full_solution[u]
        full_solution[s] = value * inv[s]
    total = full_solution[0]
    for s in range(1, HIST):
        total = total + full_solution[s]
    return [full_solution[s] / total for s in range(HIST)]


def main_kernel(
    small, sig_hist, res_hist, sig_new, res_new,
    own, own_extra, mixed_out, coef_out,
    sig_v, res_v, sign_v, resn_v, acc, weights, gx, gy, table, regroup,
    mixed, spectra, turned,
    in_sem, share_sem, s1, r1, se, s2, r2, out_sem, local_sem,
):
    k, i = lax.axis_index("ka"), lax.axis_index("wa")
    x, core = i // 2, i % 2
    z, y = k // 4, k % 4

    def each(low, high, do):
        def step(d, _):
            do(d)
            return 0

        lax.fori_loop(low, high, step, 0)

    def arrived(ref, sem):
        pltpu.make_async_copy(ref, ref, sem).wait()

    def gram_cols(n):
        return pl.ds(pl.multiple_of(n * (GRAM_STEP * 128), 128), GRAM_STEP * 128)

    def gram_reads(n):
        cols = gram_cols(n)
        return (
            pltpu.make_async_copy(res_hist.at[:, :, :, cols], res_v.at[:, :, :, cols], in_sem.at[0, n]),
            pltpu.make_async_copy(res_new.at[:, :, cols], resn_v.at[:, :, cols], in_sem.at[1, n]),
        )

    sigma_reads = []
    for n, (start, size) in enumerate(((8192, 1408), (0, 4096), (4096, 4096))):
        cols = pl.ds(start, size)
        sigma_reads.append(
            (
                pltpu.make_async_copy(sig_hist.at[:, :, :, cols], sig_v.at[:, :, :, cols], in_sem.at[2, n]),
                pltpu.make_async_copy(sig_new.at[:, :, cols], sign_v.at[:, :, cols], in_sem.at[3, n]),
            )
        )
    for n in range(GRAM_STEPS):
        for read in gram_reads(n):
            read.start()

    barrier = pltpu.get_barrier_semaphore()

    def greet_wa(d, _):
        pl.semaphore_signal(barrier, inc=1, device_id=(k, (i + d) % WA), device_id_type=MESH)
        return 0

    def greet_ka(d, _):
        pl.semaphore_signal(barrier, inc=1, device_id=((k + d) % KA, i), device_id_type=MESH)
        return 0

    lax.fori_loop(1, WA, greet_wa, 0)
    lax.fori_loop(1, KA, greet_ka, 0)

    acc[...] = jnp.zeros_like(acc)

    def add_products(n):
        for read in gram_reads(n):
            read.wait()
        cols = gram_cols(n)
        total = None
        for ri in range(2):
            block = jnp.concatenate(
                [res_v[:, ri, :, cols].reshape(HIST * ROWS, GRAM_STEP * 128), resn_v[ri, :, cols]], axis=0
            )
            product = lax.dot_general(block, block, (((1,), (1,)), ((), ())), preferred_element_type=F32)
            total = product if total is None else total + product
        acc[...] += total

    each(0, GRAM_STEPS, add_products)
    for pair in sigma_reads:
        for read in pair:
            read.start()
    rows = lax.broadcasted_iota(jnp.int32, acc.shape, 0)
    lanes = lax.broadcasted_iota(jnp.int32, acc.shape, 1)
    kept = jnp.where((rows & (ROWS - 1)) == (lanes & (ROWS - 1)), acc[...], 0.0)
    by_lane = jnp.sum(kept.reshape(7, ROWS, 7 * ROWS), axis=1)
    fold = jnp.where(
        lax.broadcasted_iota(jnp.int32, (7 * ROWS, 128), 0) // ROWS
        == lax.broadcasted_iota(jnp.int32, (7 * ROWS, 128), 1) % 16,
        1.0,
        0.0,
    )
    share = jnp.dot(by_lane, fold, preferred_element_type=F32, precision=lax.Precision.HIGHEST)
    row = lax.broadcasted_iota(jnp.int32, (7, 128), 0)
    group = lax.broadcasted_iota(jnp.int32, (7, 128), 1) // 16
    gx[i] = jnp.sum(jnp.where(row == group, share, 0.0), axis=0, keepdims=True)

    pl.semaphore_wait(barrier, WA - 1 + KA - 1)

    def share_wa(d):
        return pltpu.make_async_remote_copy(
            src_ref=gx.at[i], dst_ref=gx.at[i], send_sem=share_sem.at[0], recv_sem=share_sem.at[1],
            device_id=(k, (i + d) % WA), device_id_type=MESH)

    def share_ka(d):
        return pltpu.make_async_remote_copy(
            src_ref=gy.at[k], dst_ref=gy.at[k], send_sem=share_sem.at[2], recv_sem=share_sem.at[3],
            device_id=((k + d) % KA, i), device_id_type=MESH)

    each(1, WA, lambda d: share_wa(d).start())
    for n in range(2):
        arrived(gx.at[: WA - 1], share_sem.at[n])
    total = gx[0]
    for n in range(1, WA):
        total = total + gx[n]
    gy[k] = total
    each(1, KA, lambda d: share_ka(d).start())
    build_transform(small, table)
    build_regroup(regroup)
    for n in range(2, 4):
        arrived(gy.at[: KA - 1], share_sem.at[n])
    gram = gy[0]
    for n in range(1, KA):
        gram = gram + gy[n]

    oldest = jnp.broadcast_to(small[4:5, 0:1], (8, 128))
    coeffs = solve(gram, oldest)
    lane = lax.broadcasted_iota(jnp.int32, (8, 128), 1)
    packed = jnp.zeros((8, 128), F32)
    newest = jnp.zeros((8, 128), F32)
    for s in range(HIST):
        packed = jnp.where(lane == s, coeffs[s], packed)
        newest = jnp.where(oldest == s, coeffs[s], newest)
        weights[s] = jnp.where(oldest == s, 0.0, coeffs[s])
    weights[HIST] = newest
    coef_out[...] = packed

    def mix(unit, start):
        def rows_of(h, _):
            ri, low = h // 2, pl.multiple_of((h % 2) * 16, 16)
            for tile in range(4):
                cols = pl.ds(pl.multiple_of(start + tile * 128, 128), 128)
                at = (ri, pl.ds(low, 16), cols)
                w = weights[HIST]
                both = jnp.concatenate([w, w], axis=0)
                total = both * (sign_v[at].astype(F32) + resn_v[at].astype(F32))
                for s in range(HIST):
                    w = weights[s]
                    both = jnp.concatenate([w, w], axis=0)
                    total = total + both * (sig_v[(s, *at)].astype(F32) + res_v[(s, *at)].astype(F32))
                mixed[unit, ri, pl.ds(low, 16), tile * 128 : (tile + 1) * 128] = total.astype(BF16)
            return 0

        lax.fori_loop(0, 4, rows_of, 0)

    def unit_copy(c, d):
        j = (i + d) % WA
        return pltpu.make_async_remote_copy(
            src_ref=mixed.at[c * WA + j], dst_ref=spectra.at[c, :, i],
            send_sem=s1.at[c], recv_sem=r1.at[c], device_id=(k, j), device_id_type=MESH)

    def unit_keep(c):
        return pltpu.make_async_copy(mixed.at[c * WA + i], spectra.at[c, :, i], local_sem.at[0, c])

    def owner_of(m):
        return 2 * ((m + y) % 4) + z % 2

    def extra_copy(m):
        return pltpu.make_async_remote_copy(
            src_ref=mixed.at[2 * WA + m], dst_ref=spectra.at[2, :, i],
            send_sem=se.at[m], recv_sem=r1.at[2], device_id=(k, owner_of(m)), device_id_type=MESH)

    def extra_keep(m):
        return pltpu.make_async_copy(mixed.at[2 * WA + m], spectra.at[2, :, i], local_sem.at[0, 2])

    writes = []
    for unit, skip in [(u, 0) for u in range(18)] + [(18, 128)]:
        start = unit * UNIT if unit < 16 else EXTRA_START[unit - 16] * 128
        writes.append(
            pltpu.make_async_copy(
                mixed.at[unit, :, :, skip:UNIT],
                mixed_out.at[:, :, start + skip : start + UNIT],
                out_sem,
            )
        )

    for read in sigma_reads[0]:
        read.wait()
    for m in range(EXTRA):
        mix(2 * WA + m, EXTRA_START[m] * 128)

        @pl.when(owner_of(m) == i)
        def _(m=m):
            extra_keep(m).start()

        @pl.when(owner_of(m) != i)
        def _(m=m):
            extra_copy(m).start()

    for c in range(2):
        for read in sigma_reads[1 + c]:
            read.wait()

        def send_unit(d, c=c):
            unit = c * WA + (i + d) % WA
            mix(unit, unit * UNIT)

            @pl.when(d == WA)
            def _():
                unit_keep(c).start()

            @pl.when(d != WA)
            def _():
                unit_copy(c, d).start()

        each(1, WA + 1, send_unit)
    for write in writes:
        write.start()

    def transform(c, b):
        values = jnp.dot(
            table[pl.ds(pl.multiple_of(b * 128, 128), 128)],
            spectra[c].reshape(2 * NTAU, UNIT),
            preferred_element_type=F32,
        ).astype(BF16)
        stacked = jnp.concatenate(
            [
                jnp.concatenate(
                    [values[n * 32 : (n + 1) * 32, a * 128 : (a + 1) * 128] for a in range(4)], axis=0
                )
                for n in range(4)
            ],
            axis=1,
        )
        grouped = jnp.dot(regroup[...], stacked, preferred_element_type=F32).astype(BF16)
        for n in range(4):
            turned[c, pl.ds((4 * b + n) * WA, WA)] = grouped[:, n * 128 : (n + 1) * 128].reshape(WA, 16, 128)

    me = k * WA + i
    extra_m = (x - y + 4) % 4
    is_owner = jnp.logical_and(z % 2 == core, extra_m < EXTRA)

    def times_copy(c, n):
        d = KA * WA - 1 - n
        pk = (z + d // 32) % 4 * 4 + (y + d // 8 % 4) % 4
        pi = (x + d // 2 % 4) % 4 * 2 + (core + d % 2) % 2
        target = own_extra.at[k * EXTRA + extra_m] if c == 2 else own.at[c, me]
        return pltpu.make_async_remote_copy(
            src_ref=turned.at[c, pk * WA + pi], dst_ref=target,
            send_sem=s2.at[c], recv_sem=r2.at[c], device_id=(pk, pi), device_id_type=MESH)

    def times_keep(c):
        target = own_extra.at[k * EXTRA + extra_m] if c == 2 else own.at[c, me]
        return pltpu.make_async_copy(turned.at[c, me], target, local_sem.at[1, c])

    def send_times(c):
        def to_z(q):
            transform(c, (z + 3 - q) % 4)
            each(32 * q, 32 * (q + 1) - q // 3, lambda n: times_copy(c, n).start())

        each(0, 4, to_z)
        times_keep(c).start()

    @pl.when(is_owner)
    def _():
        extra_keep(0).wait()
        arrived(spectra.at[2, :, : WA - 1], r1.at[2])
        send_times(2)

    for c in range(2):
        unit_keep(c).wait()
        arrived(spectra.at[c, :, : WA - 1], r1.at[c])
        send_times(c)

    for m in range(EXTRA):

        @pl.when(owner_of(m) != i)
        def _(m=m):
            extra_copy(m).wait_send()

    for c in range(2):
        arrived(spectra.at[c, :, : WA - 1], s1.at[c])

    arrived(mixed_out, out_sem)

    @pl.when(is_owner)
    def _():
        times_keep(2).wait()
        arrived(turned.at[2, : KA * WA - 1], s2.at[2])
        arrived(own_extra.at[: KA * EXTRA - 1], r2.at[2])

    @pl.when(jnp.logical_not(is_owner))
    def _():
        arrived(own_extra, r2.at[2])

    for c in range(2):
        times_keep(c).wait()
        arrived(turned.at[c, : KA * WA - 1], s2.at[c])
        arrived(own.at[c, : KA * WA - 1], r2.at[c])


def last_kernel(own, own_extra, mixed, coef_in, out, mixed_out, coef_out, times, out_sem):
    passed = pltpu.make_async_copy(mixed, mixed_out, out_sem.at[4])
    passed.start()
    coef_out[...] = coef_in[0, :HIST]

    def place(value, tile):
        value = value.astype(F32)
        times[0, pl.ds(2 * tile, 8)] = value[:8]
        times[1, pl.ds(2 * tile, 8)] = value[8:]

    writes = []
    for part in range(4):

        def row(n, _, part=part):
            k = 4 * part + n
            for c in range(2):
                for i in range(WA):
                    place(own[c, k * WA + i], k * TILES + (c * WA + i) * 4)
            for m in range(EXTRA):
                place(own_extra[k * EXTRA + m], k * TILES + EXTRA_START[m])
            return 0

        lax.fori_loop(0, 4, row, 0)
        rows = pl.ds(part * 4 * TILES * 2, 4 * TILES * 2)
        writes.append(pltpu.make_async_copy(times.at[:, rows], out.at[:, rows], out_sem.at[part]))
        writes[-1].start()
    for write in writes:
        write.wait()
    passed.wait()


def shards(sigma_hist, resid_hist, sigma_new, resid_new, slot_order, freq_index, freq_weight):
    vmem = pl.BlockSpec(memory_space=pltpu.VMEM)
    hbm = pl.BlockSpec(memory_space=pltpu.HBM)
    dma = pltpu.SemaphoreType.DMA
    whole = jnp.pad(freq_index, (0, 384)) + jnp.pad(slot_order, (2 * NTAU, 128 - HIST))
    small = (whole.astype(F32) + jnp.pad(freq_weight, (NTAU, 128))).reshape(5, 128)
    own, own_extra, mixed, coeffs = pl.pallas_call(
        main_kernel,
        out_shape=(
            jax.ShapeDtypeStruct((2, KA * WA, 16, 128), BF16),
            jax.ShapeDtypeStruct((KA * EXTRA, 16, 128), BF16),
            jax.ShapeDtypeStruct(sigma_new.shape, BF16),
            jax.ShapeDtypeStruct((8, 128), F32),
        ),
        in_specs=[vmem] + [hbm] * 4,
        out_specs=(hbm, hbm, hbm, vmem),
        scratch_shapes=[
            pltpu.VMEM(sigma_hist.shape, BF16),
            pltpu.VMEM(resid_hist.shape, BF16),
            pltpu.VMEM(sigma_new.shape, BF16),
            pltpu.VMEM(resid_new.shape, BF16),
            pltpu.VMEM((7 * ROWS, 7 * ROWS), F32),
            pltpu.VMEM((HIST + 1, 8, 128), F32),
            pltpu.VMEM((WA, 1, 128), F32),
            pltpu.VMEM((KA, 1, 128), F32),
            pltpu.VMEM((2 * NTAU, 2 * NTAU), BF16),
            pltpu.VMEM((128, 128), BF16),
            pltpu.VMEM((2 * WA + EXTRA, 2, ROWS, UNIT), BF16),
            pltpu.VMEM((3, 2, WA, ROWS, UNIT), BF16),
            pltpu.VMEM((3, KA * WA, 16, 128), BF16),
            dma((4, 3)),
            dma((4,)),
            dma((2,)),
            dma((3,)),
            dma((EXTRA,)),
            dma((3,)),
            dma((3,)),
            dma,
            dma((2, 3)),
        ],
        compiler_params=pltpu.CompilerParams(
            collective_id=0, has_side_effects=True, vmem_limit_bytes=51 * 2**20
        ),
        name="mix_and_transform",
    )(small, sigma_hist, resid_hist, sigma_new, resid_new)
    out, mixed_sigma, diis_coeffs = pl.pallas_call(
        last_kernel,
        out_shape=(
            jax.ShapeDtypeStruct((2, KA * TILES * 2, 128), F32),
            jax.ShapeDtypeStruct(sigma_new.shape, BF16),
            jax.ShapeDtypeStruct((HIST,), F32),
        ),
        in_specs=[vmem] * 4,
        out_specs=(hbm, hbm, vmem),
        scratch_shapes=[
            pltpu.VMEM((2, KA * TILES * 2, 128), F32),
            dma((5,)),
        ],
        compiler_params=pltpu.CompilerParams(vmem_limit_bytes=16 * 2**20),
        name="unpack",
    )(own, own_extra, mixed, coeffs)
    sigma_tau = out.reshape(2, KA * TILES, 2, 128).transpose(0, 2, 1, 3).reshape(2, 2, KA * WIDTH)
    return (sigma_tau, mixed_sigma, diis_coeffs)


def solution(mesh):
    return jax.shard_map(
        shards,
        mesh=mesh,
        in_specs=(
            P(None, None, "wa", "ka"),
            P(None, None, "wa", "ka"),
            P(None, "wa", "ka"),
            P(None, "wa", "ka"),
            P(),
            P(),
            P(),
        ),
        out_specs=(P(("ka", "wa"), None, None), P(None, "wa", "ka"), P()),
        check_vma=False,
    )
```
